32 devices in a mesh: parts: 2 (over x), store: 8 (over z, y), head: 2 (over core).
Axes of the slice: x: 2, y: 2, z: 4, core: 2. Of those that a mesh axis runs over, the one named last changes fastest.
Arguments:
- queries: bfloat16 [128, 64, 8192], P(('parts', 'store'), None, 'head'), parts along dimension 0, may hold values from -5 to 5, as said below
- own_keys: bfloat16 [128, 64, 1024], P(('parts', 'store'), None, 'head'), parts along dimension 0, may hold values from -5 to 5, as said below
- own_values: bfloat16 [128, 64, 1024], P(('parts', 'store'), None, 'head'), parts along dimension 0, may hold values from -6 to 6
- passage_kv: bfloat16 [768, 2, 32, 1024], P(('parts', 'store', 'head')), parts along dimension 0, may hold values from -6 to 6
- passage_rows: int32 [768], P('parts'), parts along dimension 0, may hold values from 0 to 383, as said below
- retrieval: int32 [128, 16], P(('parts', 'store')), parts along dimension 0, may hold values from 0 to 383, as said below
- offsets: int32 [768], P('parts'), parts along dimension 0, may hold values from 0 to 2047
Outputs:
- attended: bfloat16 [128, 64, 8192], P(('parts', 'store'), None, 'head'), parts along dimension 0
The draws below stay inside these ranges and needn't reach their ends.
There are 2 independent parts, one for each index of `parts`. The reference program is written for one: setup_inputs(seed, part) draws one part's arguments, and reference() takes and returns one part's arrays. A program takes and returns all parts, laid end to end along the dimension named above; each array names one. Nothing has to cross between parts.
Inputs may be any that keep to these rules, and one draw needn't show every extreme that they name: queries have entries of order one. own_keys have entries of order one. `passage_rows`: A permutation of the passage ids. `retrieval`: each request names 16 different passages, and the 8 requests of one aligned block (one request group) name no passage twice. Among those 128 passages, at most 12 have their row on one device of the store (row // 24), and some device holds exactly 12 of them.
All inputs are finite; a program needn't handle non-finite values.
Results may differ from the reference program's by a relative error of at most 0.0059.
Values may be sent and summed in bfloat16 or wider, within the bound.
A program may use at most 128 MiB of HBM per device.

```python
import jax
import jax.numpy as jnp
from jax import lax

HEADS = 64
KV_HEADS = 8
HEAD_DIM = 128
NPASS = 16
QLEN = 64
PLEN = 32
REQ_DEV = 8
P_DEV = 24
REQUESTS = 64
PASSAGES = 384
CAP = 12
N_STORE = 8
N_HEAD = 2


def draw_queries(key, part):
    key = jax.random.fold_in(key, 3)
    drawn = jnp.clip(jax.random.normal(key, (REQUESTS, QLEN, HEADS * HEAD_DIM), jnp.float32), -5.0, 5.0)
    return drawn.astype(jnp.bfloat16)


def draw_own_keys(key, part):
    key = jax.random.fold_in(key, 5)
    drawn = jnp.clip(jax.random.normal(key, (REQUESTS, QLEN, KV_HEADS * HEAD_DIM), jnp.float32), -5.0, 5.0)
    return drawn.astype(jnp.bfloat16)


def fetch_plan(key):
    dev_count = N_STORE * N_HEAD
    pick_count = REQ_DEV * NPASS
    rows_perm = jax.random.permutation(jax.random.fold_in(key, 21), PASSAGES).astype(jnp.int32)
    hot_level = jax.random.randint(jax.random.fold_in(key, 22), (dev_count,), 0, 4)
    noise_vals = jax.random.randint(jax.random.fold_in(key, 23), (N_STORE, dev_count), 0, 256)
    order_score = (noise_vals + 96 * hot_level[None, :]) * dev_count + jnp.arange(dev_count)[None, :]
    dev_order = jnp.argsort(-order_score, axis=1).astype(jnp.int32)
    multiplicity = jax.random.randint(jax.random.fold_in(key, 24), (N_STORE, dev_count), (CAP + 1) // 2, CAP + 1)
    multiplicity = multiplicity.at[:, 0].set(CAP)
    end_marks = jnp.cumsum(multiplicity, axis=1)
    pick_index = jnp.arange(pick_count)
    slot_pos = jnp.sum(end_marks[:, None, :] <= pick_index[None, :, None], axis=2).astype(jnp.int32)
    device_pick = jnp.take_along_axis(dev_order, slot_pos, axis=1)
    run_start = jnp.take_along_axis(end_marks - multiplicity, slot_pos, axis=1)
    rank_in = pick_index[None, :] - run_start
    base_slot = jax.random.randint(jax.random.fold_in(key, 25), (N_STORE, dev_count), 0, P_DEV)
    slot_index = (jnp.take_along_axis(base_slot, device_pick, axis=1) + rank_in) % P_DEV
    chosen_rows = device_pick * P_DEV + slot_index
    shuffle_score = jax.random.randint(jax.random.fold_in(key, 26), (N_STORE, pick_count), 0, 65536) * pick_count + pick_index[None, :]
    shuffled = jnp.argsort(shuffle_score, axis=1)
    chosen_rows = jnp.take_along_axis(chosen_rows, shuffled, axis=1)
    inverse = jnp.argsort(rows_perm).astype(jnp.int32)
    id_lists = inverse[chosen_rows].reshape(N_STORE * REQ_DEV, NPASS)
    return (rows_perm, id_lists.astype(jnp.int32))


def draw_passage_rows(key, part):
    rows_perm, id_lists = fetch_plan(key)
    return rows_perm


def draw_retrieval(key, part):
    rows_perm, id_lists = fetch_plan(key)
    return id_lists


def touch_ends(values, key, least, high):
    shape = values.shape
    spot = [jax.random.randint(jax.random.fold_in(key, axis), (), 0, shape[axis]) for axis in range(len(shape))]
    values = values.at[tuple(spot)].set(least)
    longest = shape.index(max(shape))
    spot[longest] = (spot[longest] + 1) % shape[longest]
    return values.at[tuple(spot)].set(high)


def block_scale(key, extent, pieces, low, top_value):
    level = 1.0
    for position, shards_of in pieces:
        draws = jax.random.uniform(jax.random.fold_in(jax.random.fold_in(key, 6), position), (shards_of,), jnp.float32, low / len(pieces), top_value / len(pieces))
        level = level * jnp.repeat(jnp.exp(draws), extent[position] // shards_of).reshape((-1,) + (1,) * (len(extent) - 1 - position))
    return level


def bell_draw(own_key, dims, deviation, most, shards=(), kind=jnp.bfloat16):
    gain = block_scale(own_key, dims, shards, -0.22, 0.18) if shards else 1.0
    values = jax.random.normal(own_key, dims, jnp.float32) * deviation * gain
    return jnp.minimum(jnp.maximum(values, -most), most).astype(kind)


def setup_inputs(seed: int = 0, part: int = 0) -> dict:
    splits = jax.random.split(jax.random.key(seed), 8)
    part_splits = jax.random.split(jax.random.fold_in(splits[7], part), 8)
    return {
        "queries": draw_queries(jax.random.fold_in(jax.random.fold_in(splits[7], part), 71), part),
        "own_keys": draw_own_keys(jax.random.fold_in(jax.random.fold_in(splits[7], part), 71), part),
        "own_values": bell_draw(part_splits[2], (REQUESTS, QLEN, KV_HEADS * HEAD_DIM), 1.0, 6.0, ((0, 8), (2, 2))),
        "passage_kv": bell_draw(part_splits[3], (PASSAGES, 2, PLEN, KV_HEADS * HEAD_DIM), 1.0, 6.0, ((0, 16),)),
        "passage_rows": draw_passage_rows(jax.random.fold_in(jax.random.fold_in(splits[7], part), 71), part),
        "retrieval": draw_retrieval(jax.random.fold_in(jax.random.fold_in(splits[7], part), 71), part),
        "offsets": touch_ends(jax.random.randint(part_splits[6], (PASSAGES,), 0, 2048), jax.random.fold_in(part_splits[6], 1), 0, 2047).astype(jnp.int32),
    }


rope_theta = 1000000.0


def rerotate(page_keys, turn_by):
    count, length, width = page_keys.shape
    half_dim = HEAD_DIM // 2
    spread = page_keys.astype(jnp.float32).reshape(count, length, width // HEAD_DIM, HEAD_DIM)
    first_half = spread[..., :half_dim]
    second_half = spread[..., half_dim:]
    inverse_freq = rope_theta ** (-(jnp.arange(half_dim, dtype=jnp.float32) * 2.0) / HEAD_DIM)
    angles = turn_by.astype(jnp.float32)[:, None] * inverse_freq[None, :]
    cosine = jnp.cos(angles)[:, None, None, :]
    sine_vals = jnp.sin(angles)[:, None, None, :]
    turned = jnp.concatenate([first_half * cosine - second_half * sine_vals, second_half * cosine + first_half * sine_vals], axis=-1)
    return turned.reshape(count, length, width).astype(jnp.bfloat16)


def attend(question, key_rows, value_rows):
    qlen_here = question.shape[0]
    key_count = key_rows.shape[0]
    query_heads = question.shape[1] // HEAD_DIM
    kv_count = key_rows.shape[1] // HEAD_DIM
    group = query_heads // kv_count
    by_head = question.reshape(qlen_here, kv_count, group, HEAD_DIM).transpose(1, 2, 0, 3).reshape(kv_count, group * qlen_here, HEAD_DIM)
    key_heads = key_rows.reshape(key_count, kv_count, HEAD_DIM).transpose(1, 0, 2)
    value_heads = value_rows.reshape(key_count, kv_count, HEAD_DIM).transpose(1, 0, 2)
    row_pos = jnp.tile(jnp.arange(qlen_here), group)
    own_pos = jnp.arange(key_count) - (key_count - qlen_here)
    visible = own_pos[None, :] <= row_pos[:, None]

    def one_head(triple):
        query_block, key_block, value_block = triple
        scores = jnp.dot(query_block, key_block.T, preferred_element_type=jnp.float32) * (HEAD_DIM ** -0.5)
        scores = jnp.where(visible, scores, -jnp.inf)
        peak = jnp.max(scores, axis=1, keepdims=True)
        expo = jnp.exp(scores - peak)
        weights = (expo / jnp.sum(expo, axis=1, keepdims=True)).astype(jnp.bfloat16)
        return jnp.dot(weights, value_block, preferred_element_type=jnp.float32).astype(jnp.bfloat16)

    result = lax.map(one_head, (by_head, key_heads, value_heads))
    return result.reshape(kv_count, group, qlen_here, HEAD_DIM).transpose(2, 0, 1, 3).reshape(qlen_here, query_heads * HEAD_DIM)


def reference(queries, own_keys, own_values, passage_kv, passage_rows, retrieval, offsets):
    width = passage_kv.shape[3]

    def one_request(bundle):
        question, own_k, own_v, id_row = bundle
        store_rows = passage_rows[id_row]
        page_data = passage_kv[store_rows]
        turn_by = (jnp.arange(NPASS, dtype=jnp.int32) * PLEN - offsets[id_row]).astype(jnp.int32)
        moved = rerotate(page_data[:, 0], turn_by).reshape(NPASS * PLEN, width)
        key_rows = jnp.concatenate([moved, own_k], axis=0)
        value_rows = jnp.concatenate([page_data[:, 1].reshape(NPASS * PLEN, width), own_v], axis=0)
        return attend(question, key_rows, value_rows)

    return lax.map(one_request, (queries, own_keys, own_values, retrieval))
```

```python
import functools

import jax
import jax.numpy as jnp
from jax import lax
from jax.experimental import pallas as pl
from jax.experimental.pallas import tpu as pltpu
from jax.sharding import PartitionSpec as P

HEAD_DIM = 128
NPASS = 16
PLEN = 32
CHUNKS = 2
ROWS_AT_ONCE = 256

rope_theta = 1000000.0
EXP2_SCALE = HEAD_DIM ** (-0.5) * 1.4426950408889634


def ranks_within(owner_ids):
    count = owner_ids.shape[0]
    same_owner = owner_ids[:, None] == owner_ids[None, :]
    earlier = jnp.arange(count)[None, :] < jnp.arange(count)[:, None]
    return jnp.sum(same_owner & earlier, axis=1)


def request_table(slot_index, local_row, total):
    hits = slot_index[:, None] == jnp.arange(total)[None, :]
    return jnp.sum(jnp.where(hits, local_row[:, None], 0), axis=0)


def pack_kernel(store_count, head_count, cap, width, wanted_ref, kv_ref, *rest):
    outs, sems = rest[:-1], rest[-1]
    half = kv_ref.shape[3] // head_count
    for chunk, out_ref in enumerate(outs):
        for head in range(head_count):
            lanes = pl.ds(head * half + chunk * width, width)

            def one_slot(i, carry):
                peer = (i // cap) * head_count + head
                j = i % cap
                row = wanted_ref[peer * cap + j]
                pltpu.make_async_copy(
                    kv_ref.at[row, :, :, lanes], out_ref.at[peer, j], sems.at[chunk]
                ).start()
                return carry

            lax.fori_loop(0, store_count * cap, one_slot, 0)
    for chunk, out_ref in enumerate(outs):
        pltpu.make_async_copy(out_ref, out_ref, sems.at[chunk]).wait()


def pack(wanted, passage_kv, store_count, head_count, cap, chunks):
    width = passage_kv.shape[3] // head_count // chunks
    shape = jax.ShapeDtypeStruct((store_count * head_count, cap, 2, PLEN, width), jnp.bfloat16)
    return pl.pallas_call(
        functools.partial(pack_kernel, store_count, head_count, cap, width),
        out_shape=[shape] * chunks,
        in_specs=[
            pl.BlockSpec(memory_space=pltpu.SMEM),
            pl.BlockSpec(memory_space=pltpu.VMEM),
        ],
        out_specs=[pl.BlockSpec(memory_space=pl.ANY)] * chunks,
        scratch_shapes=[pltpu.SemaphoreType.DMA((chunks,))],
        compiler_params=pltpu.CompilerParams(vmem_limit_bytes=16 * 1024 * 1024),
    )(wanted.reshape(-1), passage_kv)


def attend_kernel(group, slot_ref, q_ref, own_k_ref, own_v_ref, cos_ref, sin_ref, *rest):
    pages = rest[:NPASS]
    out_ref = rest[-1]
    qlen = q_ref.shape[1]
    kv_count = own_k_ref.shape[2] // HEAD_DIM
    span = ROWS_AT_ONCE // qlen
    ones = jnp.ones((NPASS * PLEN + qlen, HEAD_DIM), jnp.bfloat16)
    token = lax.broadcasted_iota(jnp.int32, (ROWS_AT_ONCE, qlen), 0) % qlen
    visible = lax.broadcasted_iota(jnp.int32, (ROWS_AT_ONCE, qlen), 1) <= token
    for kv in range(kv_count):
        lanes = slice(kv * HEAD_DIM, (kv + 1) * HEAD_DIM)
        keys = []
        for j in range(NPASS):
            stored = pages[j][0, 0, :, lanes].astype(jnp.float32)
            turned = stored * cos_ref[0, j : j + 1, :] + pltpu.roll(
                stored, HEAD_DIM // 2, 1
            ) * sin_ref[0, j : j + 1, :]
            keys.append(turned.astype(jnp.bfloat16))
        keys = jnp.concatenate(keys + [own_k_ref[0, :, lanes]], axis=0)
        values = jnp.concatenate(
            [pages[j][0, 1, :, lanes] for j in range(NPASS)] + [own_v_ref[0, :, lanes]], axis=0
        )
        values = jnp.concatenate([values, ones], axis=1)
        for first in range(0, group, span):
            heads = [kv * group + first + g for g in range(span)]
            question = jnp.concatenate(
                [q_ref[0, :, h * HEAD_DIM : (h + 1) * HEAD_DIM] for h in heads], axis=0
            )
            scores = lax.dot_general(
                question, keys, (((1,), (1,)), ((), ())), preferred_element_type=jnp.float32
            )
            own = jnp.where(visible, scores[:, NPASS * PLEN :], -jnp.inf)
            scores = jnp.concatenate([scores[:, : NPASS * PLEN], own], axis=1)
            peak = jnp.max(scores, axis=1, keepdims=True)
            expo = jnp.exp2((scores - peak) * EXP2_SCALE).astype(jnp.bfloat16)
            both = jnp.dot(expo, values, preferred_element_type=jnp.float32)
            result = (both[:, :HEAD_DIM] / both[:, HEAD_DIM:]).astype(jnp.bfloat16)
            for g, h in enumerate(heads):
                out_ref[0, :, h * HEAD_DIM : (h + 1) * HEAD_DIM] = result[g * qlen : (g + 1) * qlen]


def attend(chunk, chunks, slot_index, queries, own_keys, own_values, cosine, sine, fetched, so_far):
    requests, qlen, q_width = queries.shape
    kv_width = own_keys.shape[2] // chunks
    q_part = q_width // chunks
    group = q_part // kv_width
    page = fetched.shape[1:]

    def by_chunk(r, slots):
        return (r, 0, chunk)

    def by_request(r, slots):
        return (r, 0, 0)

    def page_spec(j):
        return pl.BlockSpec((1,) + page, lambda r, slots: (slots[r * NPASS + j], 0, 0, 0))

    in_specs = [
        pl.BlockSpec((1, qlen, q_part), by_chunk),
        pl.BlockSpec((1, qlen, kv_width), by_chunk),
        pl.BlockSpec((1, qlen, kv_width), by_chunk),
        pl.BlockSpec((1, NPASS, HEAD_DIM), by_request),
        pl.BlockSpec((1, NPASS, HEAD_DIM), by_request),
    ] + [page_spec(j) for j in range(NPASS)]
    operands = [queries, own_keys, own_values, cosine, sine] + [fetched] * NPASS
    aliases = {}
    if so_far is not None:
        in_specs.append(pl.BlockSpec(memory_space=pl.ANY))
        aliases = {1 + len(operands): 0}
        operands.append(so_far)
    keys = NPASS * PLEN + qlen
    return pl.pallas_call(
        functools.partial(attend_kernel, group),
        grid_spec=pltpu.PrefetchScalarGridSpec(
            num_scalar_prefetch=1,
            grid=(requests,),
            in_specs=in_specs,
            out_specs=pl.BlockSpec((1, qlen, q_part), by_chunk),
        ),
        out_shape=jax.ShapeDtypeStruct(queries.shape, jnp.bfloat16),
        input_output_aliases=aliases,
        compiler_params=pltpu.CompilerParams(vmem_limit_bytes=40 * 1024 * 1024),
        cost_estimate=pl.CostEstimate(
            flops=6 * requests * qlen * q_part * keys,
            bytes_accessed=4 * requests * qlen * q_part + 2 * requests * NPASS * 2 * PLEN * kv_width,
            transcendentals=requests * qlen * (q_part // HEAD_DIM) * keys,
        ),
    )(slot_index, *operands)


def local(queries, own_keys, own_values, passage_kv, passage_rows, retrieval, offsets):
    stored_count = passage_kv.shape[0]
    store_count = lax.axis_size("store")
    head_count = lax.axis_size("head")
    peer_count = store_count * head_count
    requests = queries.shape[0]
    pick_ids = retrieval.reshape(-1)
    pick_count = pick_ids.shape[0]
    cap_dev = 3 * pick_count // (2 * peer_count)
    store_rows = passage_rows[pick_ids]
    owner_dev = store_rows // stored_count
    local_row = store_rows % stored_count
    slot_index = owner_dev * cap_dev + ranks_within(owner_dev)
    asked = request_table(slot_index, local_row, peer_count * cap_dev).reshape(peer_count, cap_dev)
    wanted = lax.all_to_all(asked, ("store", "head"), split_axis=0, concat_axis=0, tiled=True)
    outgoing = pack(wanted, passage_kv, store_count, head_count, cap_dev, CHUNKS)

    turn_by = jnp.arange(pick_count, dtype=jnp.int32) % NPASS * PLEN - offsets[pick_ids]
    half_dim = HEAD_DIM // 2
    inverse_freq = rope_theta ** (-(jnp.arange(half_dim, dtype=jnp.float32) * 2.0) / HEAD_DIM)
    angles = turn_by.astype(jnp.float32)[:, None] * inverse_freq[None, :]
    cosine, sine = jnp.cos(angles), jnp.sin(angles)
    cosine = jnp.concatenate([cosine, cosine], axis=1).reshape(requests, NPASS, HEAD_DIM)
    sine = jnp.concatenate([-sine, sine], axis=1).reshape(requests, NPASS, HEAD_DIM)

    result = None
    for chunk in range(CHUNKS):
        incoming = lax.all_to_all(
            outgoing[chunk], ("store", "head"), split_axis=0, concat_axis=0, tiled=True
        )
        fetched = incoming.reshape((peer_count * cap_dev,) + incoming.shape[2:])
        result = attend(
            chunk, CHUNKS, slot_index, queries, own_keys, own_values, cosine, sine, fetched, result
        )
    return result


def solution(mesh):
    in_specs = (
        P(("parts", "store"), None, "head"),
        P(("parts", "store"), None, "head"),
        P(("parts", "store"), None, "head"),
        P(("parts", "store", "head"), None, None, None),
        P("parts"),
        P(("parts", "store"), None),
        P("parts"),
    )
    out_specs = P(("parts", "store"), None, "head")
    return jax.shard_map(local, mesh=mesh, in_specs=in_specs, out_specs=out_specs, check_vma=False)
```

```python
import functools

import jax
import jax.numpy as jnp
from jax import lax
from jax.experimental import pallas as pl
from jax.experimental.pallas import tpu as pltpu
from jax.sharding import PartitionSpec as P

HEAD_DIM = 128
NPASS = 16
PLEN = 32
CHUNKS = 1
PLANE = 4
ROWS_AT_ONCE = 256

rope_theta = 1000000.0
EXP2_SCALE = HEAD_DIM ** (-0.5) * 1.4426950408889634


def ranks_within(owner_ids):
    count = owner_ids.shape[0]
    same_owner = owner_ids[:, None] == owner_ids[None, :]
    earlier = jnp.arange(count)[None, :] < jnp.arange(count)[:, None]
    return jnp.sum(same_owner & earlier, axis=1)


def request_table(slot_index, local_row, total):
    hits = slot_index[:, None] == jnp.arange(total)[None, :]
    return jnp.sum(jnp.where(hits, local_row[:, None], 0), axis=0)


def pack_kernel(store_count, head_count, cap, width, wanted_ref, kv_ref, *rest):
    outs, sems = rest[:-1], rest[-1]
    half = kv_ref.shape[3] // head_count
    for chunk, out_ref in enumerate(outs):
        for head in range(head_count):
            lanes = pl.ds(head * half + chunk * width, width)

            def one_slot(i, carry):
                peer = (i // cap) * head_count + head
                j = i % cap
                row = wanted_ref[peer * cap + j]
                pltpu.make_async_copy(
                    kv_ref.at[row, :, :, lanes], out_ref.at[peer, j], sems.at[chunk]
                ).start()
                return carry

            lax.fori_loop(0, store_count * cap, one_slot, 0)
    for chunk, out_ref in enumerate(outs):
        pltpu.make_async_copy(out_ref, out_ref, sems.at[chunk]).wait()


def pack(wanted, passage_kv, store_count, head_count, cap, chunks):
    width = passage_kv.shape[3] // head_count // chunks
    shape = jax.ShapeDtypeStruct((store_count * head_count, cap, 2, PLEN, width), jnp.bfloat16)
    return pl.pallas_call(
        functools.partial(pack_kernel, store_count, head_count, cap, width),
        out_shape=[shape] * chunks,
        in_specs=[
            pl.BlockSpec(memory_space=pltpu.SMEM),
            pl.BlockSpec(memory_space=pltpu.VMEM),
        ],
        out_specs=[pl.BlockSpec(memory_space=pl.ANY)] * chunks,
        scratch_shapes=[pltpu.SemaphoreType.DMA((chunks,))],
        compiler_params=pltpu.CompilerParams(vmem_limit_bytes=16 * 1024 * 1024),
    )(wanted.reshape(-1), passage_kv)


def attend_kernel(group, slot_ref, q_ref, own_k_ref, own_v_ref, cos_ref, sin_ref, *rest):
    pages = rest[:NPASS]
    out_ref = rest[-1]
    qlen = q_ref.shape[1]
    kv_count = own_k_ref.shape[2] // HEAD_DIM
    span = ROWS_AT_ONCE // qlen
    ones = jnp.ones((NPASS * PLEN + qlen, HEAD_DIM), jnp.bfloat16)
    token = lax.broadcasted_iota(jnp.int32, (ROWS_AT_ONCE, qlen), 0) % qlen
    visible = lax.broadcasted_iota(jnp.int32, (ROWS_AT_ONCE, qlen), 1) <= token
    for kv in range(kv_count):
        lanes = slice(kv * HEAD_DIM, (kv + 1) * HEAD_DIM)
        keys = []
        for j in range(NPASS):
            stored = pages[j][0, 0, :, lanes].astype(jnp.float32)
            turned = stored * cos_ref[0, j : j + 1, :] + pltpu.roll(
                stored, HEAD_DIM // 2, 1
            ) * sin_ref[0, j : j + 1, :]
            keys.append(turned.astype(jnp.bfloat16))
        keys = jnp.concatenate(keys + [own_k_ref[0, :, lanes]], axis=0)
        values = jnp.concatenate(
            [pages[j][0, 1, :, lanes] for j in range(NPASS)] + [own_v_ref[0, :, lanes]], axis=0
        )
        values = jnp.concatenate([values, ones], axis=1)
        for first in range(0, group, span):
            heads = [kv * group + first + g for g in range(span)]
            question = jnp.concatenate(
                [q_ref[0, :, h * HEAD_DIM : (h + 1) * HEAD_DIM] for h in heads], axis=0
            )
            scores = lax.dot_general(
                question, keys, (((1,), (1,)), ((), ())), preferred_element_type=jnp.float32
            )
            own = jnp.where(visible, scores[:, NPASS * PLEN :], -jnp.inf)
            scores = jnp.concatenate([scores[:, : NPASS * PLEN], own], axis=1)
            peak = jnp.max(scores, axis=1, keepdims=True)
            expo = jnp.exp2((scores - peak) * EXP2_SCALE).astype(jnp.bfloat16)
            both = jnp.dot(expo, values, preferred_element_type=jnp.float32)
            result = (both[:, :HEAD_DIM] / both[:, HEAD_DIM:]).astype(jnp.bfloat16)
            for g, h in enumerate(heads):
                out_ref[0, :, h * HEAD_DIM : (h + 1) * HEAD_DIM] = result[g * qlen : (g + 1) * qlen]


def attend(chunk, chunks, slot_index, queries, own_keys, own_values, cosine, sine, fetched, so_far):
    requests, qlen, q_width = queries.shape
    kv_width = own_keys.shape[2] // chunks
    q_part = q_width // chunks
    group = q_part // kv_width
    page = fetched.shape[1:]

    def by_chunk(r, slots):
        return (r, 0, chunk)

    def by_request(r, slots):
        return (r, 0, 0)

    def page_spec(j):
        return pl.BlockSpec((1,) + page, lambda r, slots: (slots[r * NPASS + j], 0, 0, 0))

    in_specs = [
        pl.BlockSpec((1, qlen, q_part), by_chunk),
        pl.BlockSpec((1, qlen, kv_width), by_chunk),
        pl.BlockSpec((1, qlen, kv_width), by_chunk),
        pl.BlockSpec((1, NPASS, HEAD_DIM), by_request),
        pl.BlockSpec((1, NPASS, HEAD_DIM), by_request),
    ] + [page_spec(j) for j in range(NPASS)]
    operands = [queries, own_keys, own_values, cosine, sine] + [fetched] * NPASS
    aliases = {}
    if so_far is not None:
        in_specs.append(pl.BlockSpec(memory_space=pl.ANY))
        aliases = {1 + len(operands): 0}
        operands.append(so_far)
    keys = NPASS * PLEN + qlen
    return pl.pallas_call(
        functools.partial(attend_kernel, group),
        grid_spec=pltpu.PrefetchScalarGridSpec(
            num_scalar_prefetch=1,
            grid=(requests,),
            in_specs=in_specs,
            out_specs=pl.BlockSpec((1, qlen, q_part), by_chunk),
        ),
        out_shape=jax.ShapeDtypeStruct(queries.shape, jnp.bfloat16),
        input_output_aliases=aliases,
        compiler_params=pltpu.CompilerParams(vmem_limit_bytes=40 * 1024 * 1024),
        cost_estimate=pl.CostEstimate(
            flops=6 * requests * qlen * q_part * keys,
            bytes_accessed=4 * requests * qlen * q_part + 2 * requests * NPASS * 2 * PLEN * kv_width,
            transcendentals=requests * qlen * (q_part // HEAD_DIM) * keys,
        ),
    )(slot_index, *operands)


def here():
    store, head = lax.axis_index("store"), lax.axis_index("head")
    return store * 2 + head, (store * 2 + head) // PLANE, (store * 2 + head) % PLANE


def remote(src, dst, send_sem, recv_sem, peer):
    return pltpu.make_async_remote_copy(
        src_ref=src,
        dst_ref=dst,
        send_sem=send_sem,
        recv_sem=recv_sem,
        device_id={"store": peer // 2, "head": peer % 2},
        device_id_type=pl.DeviceIdType.MESH,
    )


def greet_all(me, count):
    barrier = pltpu.get_barrier_semaphore()

    def greet(k, carry):
        peer = (me + k) % count
        pl.semaphore_signal(
            barrier,
            inc=1,
            device_id={"store": peer // 2, "head": peer % 2},
            device_id_type=pl.DeviceIdType.MESH,
        )
        return carry

    lax.fori_loop(1, count, greet, 0)
    pl.semaphore_wait(barrier, count - 1)


def near_kernel(out_ref, kv_ref, in_ref, relay_ref, send, recv, keep):
    me, plane, spot = here()
    outer = (plane == 0) | (plane == 3)
    inner = (plane == 1) | (plane == 2)
    greet_all(me, 4 * PLANE)
    whole = remote(
        kv_ref, relay_ref, send.at[8], recv.at[8], jnp.where(plane == 0, 2, 1) * PLANE + spot
    )

    def block(k, target_plane):
        peer = target_plane * PLANE + (spot + k % PLANE) % PLANE
        return remote(out_ref.at[peer], in_ref.at[me], send.at[k], recv.at[k], peer)

    out_plane = jnp.where(plane == 1, 0, 3)

    @pl.when(outer)
    def _():
        whole.start()

    @pl.when(inner)
    def _():
        for k in range(PLANE):
            block(PLANE + k, out_plane).start()

    for k in range(1, PLANE):
        block(k, plane).start()
    own = pltpu.make_async_copy(out_ref.at[me], in_ref.at[me], keep)
    own.start()
    own.wait()
    for k in range(1, PLANE):
        block(k, plane).wait()

    @pl.when(outer)
    def _():
        for k in range(PLANE):
            block(PLANE + k, plane).wait_recv()
        whole.wait_send()

    @pl.when(inner)
    def _():
        for k in range(PLANE):
            block(PLANE + k, out_plane).wait_send()
        whole.wait_recv()


def far_kernel(out_ref, relay_ref, have_ref, in_ref, send, recv, keep):
    me, plane, spot = here()
    outer = (plane == 0) | (plane == 3)
    inner = (plane == 1) | (plane == 2)
    greet_all(me, 4 * PLANE)
    origin = jnp.where(plane == 2, 0, 3) * PLANE + spot

    def block(k, target_plane):
        peer = target_plane * PLANE + (spot + k % PLANE) % PLANE
        return remote(out_ref.at[peer], in_ref.at[me], send.at[k], recv.at[k], peer)

    def relayed(k, step, target_plane):
        spot_there = (spot + k % PLANE) % PLANE
        return remote(
            relay_ref.at[step, spot_there],
            in_ref.at[origin],
            send.at[k],
            recv.at[k],
            target_plane * PLANE + spot_there,
        )

    inward = jnp.where(plane == 0, 1, 2)
    across = jnp.where(plane == 1, 2, 1)
    beyond = jnp.where(plane == 1, 3, 0)
    out_plane = jnp.where(plane == 1, 0, 3)
    own = pltpu.make_async_copy(relay_ref.at[0, spot], in_ref.at[origin], keep)

    @pl.when(outer)
    def _():
        for k in range(PLANE):
            block(k, inward).start()
        for k in range(PLANE):
            block(k, inward).wait_send()
        for k in range(PLANE):
            block(2 * PLANE + k, inward).wait_recv()
            relayed(4 * PLANE + k, 1, inward).wait_recv()

    @pl.when(inner)
    def _():
        for k in range(PLANE):
            block(2 * PLANE + k, beyond).start()
            relayed(4 * PLANE + k, 1, out_plane).start()
            block(PLANE + k, across).start()
        for k in range(1, PLANE):
            relayed(3 * PLANE + k, 0, plane).start()
        own.start()
        own.wait()
        for k in range(PLANE):
            block(2 * PLANE + k, beyond).wait_send()
            relayed(4 * PLANE + k, 1, out_plane).wait_send()
            block(PLANE + k, across).wait()
            block(k, across).wait_recv()
        for k in range(1, PLANE):
            relayed(3 * PLANE + k, 0, plane).wait()


def exchange(wanted_all, outgoing, passage_kv):
    any_space = pl.BlockSpec(memory_space=pl.ANY)
    incoming, relay = pl.pallas_call(
        near_kernel,
        out_shape=[
            jax.ShapeDtypeStruct(outgoing.shape, jnp.bfloat16),
            jax.ShapeDtypeStruct(passage_kv.shape, jnp.bfloat16),
        ],
        in_specs=[any_space] * 2,
        out_specs=[any_space] * 2,
        scratch_shapes=[
            pltpu.SemaphoreType.DMA((9,)),
            pltpu.SemaphoreType.DMA((9,)),
            pltpu.SemaphoreType.DMA,
        ],
        compiler_params=pltpu.CompilerParams(collective_id=1, has_side_effects=True),
    )(outgoing, passage_kv)
    me, plane, spot = here()
    origin = jnp.where(plane == 2, 0, 3) * PLANE + spot
    for_origin = lax.dynamic_index_in_dim(wanted_all, origin, 1, keepdims=False)
    cap = for_origin.shape[1]
    by_plane = for_origin.reshape(4, 2, cap)
    out_plane = jnp.where(plane == 1, 0, 3)
    lists = jnp.concatenate(
        [
            lax.dynamic_index_in_dim(by_plane, plane, 0, keepdims=False),
            lax.dynamic_index_in_dim(by_plane, out_plane, 0, keepdims=False),
        ],
        axis=0,
    )
    lists = jnp.repeat(lists, 2, axis=0)
    relay_out = pack(lists, relay, 4, 2, cap, 1)[0]
    relay_out = relay_out.reshape((2, PLANE) + relay_out.shape[1:])
    return pl.pallas_call(
        far_kernel,
        out_shape=jax.ShapeDtypeStruct(outgoing.shape, jnp.bfloat16),
        in_specs=[any_space] * 3,
        out_specs=any_space,
        input_output_aliases={2: 0},
        scratch_shapes=[
            pltpu.SemaphoreType.DMA((5 * PLANE,)),
            pltpu.SemaphoreType.DMA((5 * PLANE,)),
            pltpu.SemaphoreType.DMA,
        ],
        compiler_params=pltpu.CompilerParams(collective_id=2, has_side_effects=True),
    )(outgoing, relay_out, incoming)


def local(queries, own_keys, own_values, passage_kv, passage_rows, retrieval, offsets):
    stored_count = passage_kv.shape[0]
    store_count = lax.axis_size("store")
    head_count = lax.axis_size("head")
    peer_count = store_count * head_count
    requests = queries.shape[0]
    pick_ids = retrieval.reshape(-1)
    pick_count = pick_ids.shape[0]
    cap_dev = 3 * pick_count // (2 * peer_count)
    store_rows = passage_rows[pick_ids]
    owner_dev = store_rows // stored_count
    local_row = store_rows % stored_count
    slot_index = owner_dev * cap_dev + ranks_within(owner_dev)
    asked = request_table(slot_index, local_row, peer_count * cap_dev).reshape(peer_count, cap_dev)
    relays = store_count == 8 and head_count == 2 and 2 * cap_dev >= stored_count
    if relays:
        told = jnp.broadcast_to(asked[None], (peer_count,) + asked.shape)
        told = lax.all_to_all(told, ("store", "head"), split_axis=0, concat_axis=0, tiled=True)
        wanted_all = told.reshape(store_count, head_count, peer_count, cap_dev)[:, 0]
        wanted = jnp.repeat(wanted_all[:, here()[0]], head_count, axis=0)
    else:
        wanted = lax.all_to_all(asked, ("store", "head"), split_axis=0, concat_axis=0, tiled=True)
    outgoing = pack(wanted, passage_kv, store_count, head_count, cap_dev, CHUNKS)

    turn_by = jnp.arange(pick_count, dtype=jnp.int32) % NPASS * PLEN - offsets[pick_ids]
    half_dim = HEAD_DIM // 2
    inverse_freq = rope_theta ** (-(jnp.arange(half_dim, dtype=jnp.float32) * 2.0) / HEAD_DIM)
    angles = turn_by.astype(jnp.float32)[:, None] * inverse_freq[None, :]
    cosine, sine = jnp.cos(angles), jnp.sin(angles)
    cosine = jnp.concatenate([cosine, cosine], axis=1).reshape(requests, NPASS, HEAD_DIM)
    sine = jnp.concatenate([-sine, sine], axis=1).reshape(requests, NPASS, HEAD_DIM)

    result = None
    for chunk in range(CHUNKS):
        if relays:
            incoming = exchange(wanted_all, outgoing[chunk], passage_kv)
        else:
            incoming = lax.all_to_all(
                outgoing[chunk], ("store", "head"), split_axis=0, concat_axis=0, tiled=True
            )
        fetched = incoming.reshape((peer_count * cap_dev,) + incoming.shape[2:])
        result = attend(
            chunk, CHUNKS, slot_index, queries, own_keys, own_values, cosine, sine, fetched, result
        )
    return result


def solution(mesh):
    in_specs = (
        P(("parts", "store"), None, "head"),
        P(("parts", "store"), None, "head"),
        P(("parts", "store"), None, "head"),
        P(("parts", "store", "head"), None, None, None),
        P("parts"),
        P(("parts", "store"), None),
        P("parts"),
    )
    out_specs = P(("parts", "store"), None, "head")
    return jax.shard_map(local, mesh=mesh, in_specs=in_specs, out_specs=out_specs, check_vma=False)
```

```python
import functools

import jax
import jax.numpy as jnp
from jax import lax
from jax.experimental import pallas as pl
from jax.experimental.pallas import tpu as pltpu
from jax.sharding import PartitionSpec as P

HEAD_DIM = 128
NPASS = 16
PLEN = 32
CHUNKS = 1
PLANE = 4
VMEM_LIMIT = 60 * 1024 * 1024
ROWS_AT_ONCE = 256

rope_theta = 1000000.0
EXP2_SCALE = HEAD_DIM ** (-0.5) * 1.4426950408889634


def ranks_within(owner_ids):
    count = owner_ids.shape[0]
    same_owner = owner_ids[:, None] == owner_ids[None, :]
    earlier = jnp.arange(count)[None, :] < jnp.arange(count)[:, None]
    return jnp.sum(same_owner & earlier, axis=1)


def request_table(slot_index, local_row, total):
    hits = slot_index[:, None] == jnp.arange(total)[None, :]
    return jnp.sum(jnp.where(hits, local_row[:, None], 0), axis=0)


def pack_kernel(store_count, head_count, cap, width, wanted_ref, kv_ref, *rest):
    outs, sems = rest[:-1], rest[-1]
    half = kv_ref.shape[3] // head_count
    for chunk, out_ref in enumerate(outs):
        for head in range(head_count):
            lanes = pl.ds(head * half + chunk * width, width)

            def one_slot(i, carry):
                peer = (i // cap) * head_count + head
                j = i % cap
                row = wanted_ref[peer * cap + j]
                pltpu.make_async_copy(
                    kv_ref.at[row, :, :, lanes], out_ref.at[peer, j], sems.at[chunk]
                ).start()
                return carry

            lax.fori_loop(0, store_count * cap, one_slot, 0)
    for chunk, out_ref in enumerate(outs):
        pltpu.make_async_copy(out_ref, out_ref, sems.at[chunk]).wait()


def pack(wanted, passage_kv, store_count, head_count, cap, chunks):
    width = passage_kv.shape[3] // head_count // chunks
    shape = jax.ShapeDtypeStruct((store_count * head_count, cap, 2, PLEN, width), jnp.bfloat16)
    return pl.pallas_call(
        functools.partial(pack_kernel, store_count, head_count, cap, width),
        out_shape=[shape] * chunks,
        in_specs=[
            pl.BlockSpec(memory_space=pltpu.SMEM),
            pl.BlockSpec(memory_space=pltpu.VMEM),
        ],
        out_specs=[pl.BlockSpec(memory_space=pl.ANY)] * chunks,
        scratch_shapes=[pltpu.SemaphoreType.DMA((chunks,))],
        compiler_params=pltpu.CompilerParams(vmem_limit_bytes=VMEM_LIMIT),
    )(wanted.reshape(-1), passage_kv)


def attend_kernel(group, slot_ref, q_ref, own_k_ref, own_v_ref, cos_ref, sin_ref, *rest):
    pages = rest[:NPASS]
    out_ref = rest[-1]
    qlen = q_ref.shape[1]
    kv_count = own_k_ref.shape[2] // HEAD_DIM
    span = ROWS_AT_ONCE // qlen
    ones = jnp.ones((NPASS * PLEN + qlen, HEAD_DIM), jnp.bfloat16)
    token = lax.broadcasted_iota(jnp.int32, (ROWS_AT_ONCE, qlen), 0) % qlen
    visible = lax.broadcasted_iota(jnp.int32, (ROWS_AT_ONCE, qlen), 1) <= token
    for kv in range(kv_count):
        lanes = slice(kv * HEAD_DIM, (kv + 1) * HEAD_DIM)
        keys = []
        for j in range(NPASS):
            stored = pages[j][0, 0, :, lanes].astype(jnp.float32)
            turned = stored * cos_ref[0, j : j + 1, :] + pltpu.roll(
                stored, HEAD_DIM // 2, 1
            ) * sin_ref[0, j : j + 1, :]
            keys.append(turned.astype(jnp.bfloat16))
        keys = jnp.concatenate(keys + [own_k_ref[0, :, lanes]], axis=0)
        values = jnp.concatenate(
            [pages[j][0, 1, :, lanes] for j in range(NPASS)] + [own_v_ref[0, :, lanes]], axis=0
        )
        values = jnp.concatenate([values, ones], axis=1)
        for first in range(0, group, span):
            heads = [kv * group + first + g for g in range(span)]
            question = jnp.concatenate(
                [q_ref[0, :, h * HEAD_DIM : (h + 1) * HEAD_DIM] for h in heads], axis=0
            )
            scores = lax.dot_general(
                question, keys, (((1,), (1,)), ((), ())), preferred_element_type=jnp.float32
            )
            own = jnp.where(visible, scores[:, NPASS * PLEN :], -jnp.inf)
            scores = jnp.concatenate([scores[:, : NPASS * PLEN], own], axis=1)
            peak = jnp.max(scores, axis=1, keepdims=True)
            expo = jnp.exp2((scores - peak) * EXP2_SCALE).astype(jnp.bfloat16)
            both = jnp.dot(expo, values, preferred_element_type=jnp.float32)
            result = (both[:, :HEAD_DIM] / both[:, HEAD_DIM:]).astype(jnp.bfloat16)
            for g, h in enumerate(heads):
                out_ref[0, :, h * HEAD_DIM : (h + 1) * HEAD_DIM] = result[g * qlen : (g + 1) * qlen]


def attend(chunk, chunks, slot_index, queries, own_keys, own_values, cosine, sine, fetched, so_far):
    requests, qlen, q_width = queries.shape
    kv_width = own_keys.shape[2] // chunks
    q_part = q_width // chunks
    group = q_part // kv_width
    page = fetched.shape[1:]

    def by_chunk(r, slots):
        return (r, 0, chunk)

    def by_request(r, slots):
        return (r, 0, 0)

    def page_spec(j):
        return pl.BlockSpec((1,) + page, lambda r, slots: (slots[r * NPASS + j], 0, 0, 0))

    in_specs = [
        pl.BlockSpec((1, qlen, q_part), by_chunk),
        pl.BlockSpec((1, qlen, kv_width), by_chunk),
        pl.BlockSpec((1, qlen, kv_width), by_chunk),
        pl.BlockSpec((1, NPASS, HEAD_DIM), by_request),
        pl.BlockSpec((1, NPASS, HEAD_DIM), by_request),
    ] + [page_spec(j) for j in range(NPASS)]
    operands = [queries, own_keys, own_values, cosine, sine] + [fetched] * NPASS
    aliases = {}
    if so_far is not None:
        in_specs.append(pl.BlockSpec(memory_space=pl.ANY))
        aliases = {1 + len(operands): 0}
        operands.append(so_far)
    keys = NPASS * PLEN + qlen
    return pl.pallas_call(
        functools.partial(attend_kernel, group),
        grid_spec=pltpu.PrefetchScalarGridSpec(
            num_scalar_prefetch=1,
            grid=(requests,),
            in_specs=in_specs,
            out_specs=pl.BlockSpec((1, qlen, q_part), by_chunk),
        ),
        out_shape=jax.ShapeDtypeStruct(queries.shape, jnp.bfloat16),
        input_output_aliases=aliases,
        compiler_params=pltpu.CompilerParams(vmem_limit_bytes=VMEM_LIMIT),
        cost_estimate=pl.CostEstimate(
            flops=6 * requests * qlen * q_part * keys,
            bytes_accessed=4 * requests * qlen * q_part + 2 * requests * NPASS * 2 * PLEN * kv_width,
            transcendentals=requests * qlen * (q_part // HEAD_DIM) * keys,
        ),
    )(slot_index, *operands)


def here():
    store, head = lax.axis_index("store"), lax.axis_index("head")
    return store * 2 + head, (store * 2 + head) // PLANE, (store * 2 + head) % PLANE


def remote(src, dst, send_sem, recv_sem, peer):
    return pltpu.make_async_remote_copy(
        src_ref=src,
        dst_ref=dst,
        send_sem=send_sem,
        recv_sem=recv_sem,
        device_id={"store": peer // 2, "head": peer % 2},
        device_id_type=pl.DeviceIdType.MESH,
    )


def greet_all(me, count):
    barrier = pltpu.get_barrier_semaphore()

    def greet(k, carry):
        peer = (me + k) % count
        pl.semaphore_signal(
            barrier,
            inc=1,
            device_id={"store": peer // 2, "head": peer % 2},
            device_id_type=pl.DeviceIdType.MESH,
        )
        return carry

    lax.fori_loop(1, count, greet, 0)
    pl.semaphore_wait(barrier, count - 1)


def near_kernel(out_ref, in_ref, send, recv, keep):
    me, plane, spot = here()
    outer = (plane == 0) | (plane == 3)
    inner = (plane == 1) | (plane == 2)
    greet_all(me, 4 * PLANE)
    def block(k, target_plane):
        peer = target_plane * PLANE + (spot + k % PLANE) % PLANE
        return remote(out_ref.at[peer], in_ref.at[me], send.at[k], recv.at[k], peer)

    out_plane = jnp.where(plane == 1, 0, 3)

    @pl.when(inner)
    def _():
        for k in range(PLANE):
            block(PLANE + k, out_plane).start()

    for k in range(1, PLANE):
        block(k, plane).start()
    own = pltpu.make_async_copy(out_ref.at[me], in_ref.at[me], keep)
    own.start()
    own.wait()
    for k in range(1, PLANE):
        block(k, plane).wait()

    @pl.when(outer)
    def _():
        for k in range(PLANE):
            block(PLANE + k, plane).wait_recv()

    @pl.when(inner)
    def _():
        for k in range(PLANE):
            block(PLANE + k, out_plane).wait_send()


def far_kernel(out_ref, relay_ref, have_ref, in_ref, send, recv, keep):
    me, plane, spot = here()
    outer = (plane == 0) | (plane == 3)
    inner = (plane == 1) | (plane == 2)
    greet_all(me, 4 * PLANE)
    origin = jnp.where(plane == 2, 0, 3) * PLANE + spot

    def block(k, target_plane):
        peer = target_plane * PLANE + (spot + k % PLANE) % PLANE
        return remote(out_ref.at[peer], in_ref.at[me], send.at[k], recv.at[k], peer)

    def relayed(k, step, target_plane):
        spot_there = (spot + k % PLANE) % PLANE
        return remote(
            relay_ref.at[step, spot_there],
            in_ref.at[origin],
            send.at[k],
            recv.at[k],
            target_plane * PLANE + spot_there,
        )

    inward = jnp.where(plane == 0, 1, 2)
    across = jnp.where(plane == 1, 2, 1)
    beyond = jnp.where(plane == 1, 3, 0)
    out_plane = jnp.where(plane == 1, 0, 3)
    own = pltpu.make_async_copy(relay_ref.at[0, spot], in_ref.at[origin], keep)

    @pl.when(outer)
    def _():
        for k in range(PLANE):
            block(k, inward).start()
        for k in range(PLANE):
            block(k, inward).wait_send()
        for k in range(PLANE):
            block(2 * PLANE + k, inward).wait_recv()
            relayed(4 * PLANE + k, 1, inward).wait_recv()

    @pl.when(inner)
    def _():
        for k in range(PLANE):
            block(2 * PLANE + k, beyond).start()
            relayed(4 * PLANE + k, 1, out_plane).start()
            block(PLANE + k, across).start()
        for k in range(1, PLANE):
            relayed(3 * PLANE + k, 0, plane).start()
        own.start()
        own.wait()
        for k in range(PLANE):
            block(2 * PLANE + k, beyond).wait_send()
            relayed(4 * PLANE + k, 1, out_plane).wait_send()
            block(PLANE + k, across).wait()
            block(k, across).wait_recv()
        for k in range(1, PLANE):
            relayed(3 * PLANE + k, 0, plane).wait()


def exchange(wanted_all, outgoing, relay):
    any_space = pl.BlockSpec(memory_space=pl.ANY)
    incoming = pl.pallas_call(
        near_kernel,
        out_shape=jax.ShapeDtypeStruct(outgoing.shape, jnp.bfloat16),
        in_specs=[any_space],
        out_specs=any_space,
        scratch_shapes=[
            pltpu.SemaphoreType.DMA((2 * PLANE,)),
            pltpu.SemaphoreType.DMA((2 * PLANE,)),
            pltpu.SemaphoreType.DMA,
        ],
        compiler_params=pltpu.CompilerParams(collective_id=1, has_side_effects=True, vmem_limit_bytes=VMEM_LIMIT),
    )(outgoing)
    me, plane, spot = here()
    origin = jnp.where(plane == 2, 0, 3) * PLANE + spot
    for_origin = lax.dynamic_index_in_dim(wanted_all, origin, 1, keepdims=False)
    cap = for_origin.shape[1]
    by_plane = for_origin.reshape(4, 2, cap)
    out_plane = jnp.where(plane == 1, 0, 3)
    lists = jnp.concatenate(
        [
            lax.dynamic_index_in_dim(by_plane, plane, 0, keepdims=False),
            lax.dynamic_index_in_dim(by_plane, out_plane, 0, keepdims=False),
        ],
        axis=0,
    )
    lists = jnp.repeat(lists, 2, axis=0)
    relay_out = pack(lists, relay, 4, 2, cap, 1)[0]
    relay_out = relay_out.reshape((2, PLANE) + relay_out.shape[1:])
    return pl.pallas_call(
        far_kernel,
        out_shape=jax.ShapeDtypeStruct(outgoing.shape, jnp.bfloat16),
        in_specs=[any_space] * 3,
        out_specs=any_space,
        input_output_aliases={2: 0},
        scratch_shapes=[
            pltpu.SemaphoreType.DMA((5 * PLANE,)),
            pltpu.SemaphoreType.DMA((5 * PLANE,)),
            pltpu.SemaphoreType.DMA,
        ],
        compiler_params=pltpu.CompilerParams(collective_id=2, has_side_effects=True, vmem_limit_bytes=VMEM_LIMIT),
    )(outgoing, relay_out, incoming)


def local(queries, own_keys, own_values, passage_kv, passage_rows, retrieval, offsets):
    stored_count = passage_kv.shape[0]
    store_count = lax.axis_size("store")
    head_count = lax.axis_size("head")
    peer_count = store_count * head_count
    requests = queries.shape[0]
    pick_ids = retrieval.reshape(-1)
    pick_count = pick_ids.shape[0]
    cap_dev = 3 * pick_count // (2 * peer_count)
    store_rows = passage_rows[pick_ids]
    owner_dev = store_rows // stored_count
    local_row = store_rows % stored_count
    slot_index = owner_dev * cap_dev + ranks_within(owner_dev)
    asked = request_table(slot_index, local_row, peer_count * cap_dev).reshape(peer_count, cap_dev)
    relays = store_count == 8 and head_count == 2 and 2 * cap_dev >= stored_count
    if relays:
        hops = [(spot, 2 * PLANE + spot) for spot in range(PLANE)]
        hops += [(3 * PLANE + spot, PLANE + spot) for spot in range(PLANE)]
        relay = lax.ppermute(passage_kv, ("store", "head"), hops)
        told = jnp.broadcast_to(asked[None], (peer_count,) + asked.shape)
        told = lax.all_to_all(told, ("store", "head"), split_axis=0, concat_axis=0, tiled=True)
        wanted_all = told.reshape(store_count, head_count, peer_count, cap_dev)[:, 0]
        wanted = jnp.repeat(wanted_all[:, here()[0]], head_count, axis=0)
    else:
        wanted = lax.all_to_all(asked, ("store", "head"), split_axis=0, concat_axis=0, tiled=True)
    outgoing = pack(wanted, passage_kv, store_count, head_count, cap_dev, CHUNKS)

    turn_by = jnp.arange(pick_count, dtype=jnp.int32) % NPASS * PLEN - offsets[pick_ids]
    half_dim = HEAD_DIM // 2
    inverse_freq = rope_theta ** (-(jnp.arange(half_dim, dtype=jnp.float32) * 2.0) / HEAD_DIM)
    angles = turn_by.astype(jnp.float32)[:, None] * inverse_freq[None, :]
    cosine, sine = jnp.cos(angles), jnp.sin(angles)
    cosine = jnp.concatenate([cosine, cosine], axis=1).reshape(requests, NPASS, HEAD_DIM)
    sine = jnp.concatenate([-sine, sine], axis=1).reshape(requests, NPASS, HEAD_DIM)

    result = None
    for chunk in range(CHUNKS):
        if relays:
            incoming = exchange(wanted_all, outgoing[chunk], relay)
        else:
            incoming = lax.all_to_all(
                outgoing[chunk], ("store", "head"), split_axis=0, concat_axis=0, tiled=True
            )
        fetched = incoming.reshape((peer_count * cap_dev,) + incoming.shape[2:])
        result = attend(
            chunk, CHUNKS, slot_index, queries, own_keys, own_values, cosine, sine, fetched, result
        )
    return result


def solution(mesh):
    in_specs = (
        P(("parts", "store"), None, "head"),
        P(("parts", "store"), None, "head"),
        P(("parts", "store"), None, "head"),
        P(("parts", "store", "head"), None, None, None),
        P("parts"),
        P(("parts", "store"), None),
        P("parts"),
    )
    out_specs = P(("parts", "store"), None, "head")
    return jax.shard_map(local, mesh=mesh, in_specs=in_specs, out_specs=out_specs, check_vma=False)
```

```python
import functools

import jax
import jax.numpy as jnp
from jax import lax
from jax.experimental import pallas as pl
from jax.experimental.pallas import tpu as pltpu
from jax.sharding import PartitionSpec as P

HEAD_DIM = 128
NPASS = 16
PLEN = 32
CHUNKS = 1
PLANE = 4
VMEM_LIMIT = 60 * 1024 * 1024
ROWS_AT_ONCE = 256

rope_theta = 1000000.0
EXP2_SCALE = HEAD_DIM ** (-0.5) * 1.4426950408889634


def ranks_within(owner_ids):
    count = owner_ids.shape[0]
    same_owner = owner_ids[:, None] == owner_ids[None, :]
    earlier = jnp.arange(count)[None, :] < jnp.arange(count)[:, None]
    return jnp.sum(same_owner & earlier, axis=1)


def request_table(slot_index, local_row, total):
    hits = slot_index[:, None] == jnp.arange(total)[None, :]
    return jnp.sum(jnp.where(hits, local_row[:, None], 0), axis=0)


def pack_kernel(store_count, head_count, cap, width, wanted_ref, kv_ref, *rest):
    outs, sems = rest[:-1], rest[-1]
    half = kv_ref.shape[3] // head_count
    for chunk, out_ref in enumerate(outs):
        for head in range(head_count):
            lanes = pl.ds(head * half + chunk * width, width)

            def one_slot(i, carry):
                peer = (i // cap) * head_count + head
                j = i % cap
                row = wanted_ref[peer * cap + j]
                pltpu.make_async_copy(
                    kv_ref.at[row, :, :, lanes], out_ref.at[peer, j], sems.at[chunk]
                ).start()
                return carry

            lax.fori_loop(0, store_count * cap, one_slot, 0)
    for chunk, out_ref in enumerate(outs):
        pltpu.make_async_copy(out_ref, out_ref, sems.at[chunk]).wait()


def pack(wanted, passage_kv, store_count, head_count, cap, chunks):
    width = passage_kv.shape[3] // head_count // chunks
    shape = jax.ShapeDtypeStruct((store_count * head_count, cap, 2, PLEN, width), jnp.bfloat16)
    return pl.pallas_call(
        functools.partial(pack_kernel, store_count, head_count, cap, width),
        out_shape=[shape] * chunks,
        in_specs=[
            pl.BlockSpec(memory_space=pltpu.SMEM),
            pl.BlockSpec(memory_space=pltpu.VMEM),
        ],
        out_specs=[pl.BlockSpec(memory_space=pl.ANY)] * chunks,
        scratch_shapes=[pltpu.SemaphoreType.DMA((chunks,))],
        compiler_params=pltpu.CompilerParams(vmem_limit_bytes=VMEM_LIMIT),
    )(wanted.reshape(-1), passage_kv)


def attend_kernel(group, slot_ref, q_ref, own_k_ref, own_v_ref, cos_ref, sin_ref, *rest):
    pages = rest[:NPASS]
    out_ref = rest[-1]
    qlen = q_ref.shape[1]
    kv_count = own_k_ref.shape[2] // HEAD_DIM
    span = ROWS_AT_ONCE // qlen
    ones = jnp.ones((NPASS * PLEN + qlen, HEAD_DIM), jnp.bfloat16)
    token = lax.broadcasted_iota(jnp.int32, (ROWS_AT_ONCE, qlen), 0) % qlen
    visible = lax.broadcasted_iota(jnp.int32, (ROWS_AT_ONCE, qlen), 1) <= token
    for kv in range(kv_count):
        lanes = slice(kv * HEAD_DIM, (kv + 1) * HEAD_DIM)
        keys = []
        for j in range(NPASS):
            stored = pages[j][0, 0, :, lanes].astype(jnp.float32)
            turned = stored * cos_ref[0, j : j + 1, :] + pltpu.roll(
                stored, HEAD_DIM // 2, 1
            ) * sin_ref[0, j : j + 1, :]
            keys.append(turned.astype(jnp.bfloat16))
        keys = jnp.concatenate(keys + [own_k_ref[0, :, lanes]], axis=0)
        values = jnp.concatenate(
            [pages[j][0, 1, :, lanes] for j in range(NPASS)] + [own_v_ref[0, :, lanes]], axis=0
        )
        values = jnp.concatenate([values, ones], axis=1)
        for first in range(0, group, span):
            heads = [kv * group + first + g for g in range(span)]
            question = jnp.concatenate(
                [q_ref[0, :, h * HEAD_DIM : (h + 1) * HEAD_DIM] for h in heads], axis=0
            )
            scores = lax.dot_general(
                question, keys, (((1,), (1,)), ((), ())), preferred_element_type=jnp.float32
            )
            own = jnp.where(visible, scores[:, NPASS * PLEN :], -jnp.inf)
            scores = jnp.concatenate([scores[:, : NPASS * PLEN], own], axis=1)
            peak = jnp.max(scores, axis=1, keepdims=True)
            expo = jnp.exp2((scores - peak) * EXP2_SCALE).astype(jnp.bfloat16)
            both = jnp.dot(expo, values, preferred_element_type=jnp.float32)
            result = (both[:, :HEAD_DIM] / both[:, HEAD_DIM:]).astype(jnp.bfloat16)
            for g, h in enumerate(heads):
                out_ref[0, :, h * HEAD_DIM : (h + 1) * HEAD_DIM] = result[g * qlen : (g + 1) * qlen]


def attend(chunk, chunks, slot_index, queries, own_keys, own_values, cosine, sine, fetched, so_far):
    requests, qlen, q_width = queries.shape
    kv_width = own_keys.shape[2] // chunks
    q_part = q_width // chunks
    group = q_part // kv_width
    page = fetched.shape[1:]

    def by_chunk(r, slots):
        return (r, 0, chunk)

    def by_request(r, slots):
        return (r, 0, 0)

    def page_spec(j):
        return pl.BlockSpec((1,) + page, lambda r, slots: (slots[r * NPASS + j], 0, 0, 0))

    in_specs = [
        pl.BlockSpec((1, qlen, q_part), by_chunk),
        pl.BlockSpec((1, qlen, kv_width), by_chunk),
        pl.BlockSpec((1, qlen, kv_width), by_chunk),
        pl.BlockSpec((1, NPASS, HEAD_DIM), by_request),
        pl.BlockSpec((1, NPASS, HEAD_DIM), by_request),
    ] + [page_spec(j) for j in range(NPASS)]
    operands = [queries, own_keys, own_values, cosine, sine] + [fetched] * NPASS
    aliases = {}
    if so_far is not None:
        in_specs.append(pl.BlockSpec(memory_space=pl.ANY))
        aliases = {1 + len(operands): 0}
        operands.append(so_far)
    keys = NPASS * PLEN + qlen
    return pl.pallas_call(
        functools.partial(attend_kernel, group),
        grid_spec=pltpu.PrefetchScalarGridSpec(
            num_scalar_prefetch=1,
            grid=(requests,),
            in_specs=in_specs,
            out_specs=pl.BlockSpec((1, qlen, q_part), by_chunk),
        ),
        out_shape=jax.ShapeDtypeStruct(queries.shape, jnp.bfloat16),
        input_output_aliases=aliases,
        compiler_params=pltpu.CompilerParams(vmem_limit_bytes=VMEM_LIMIT),
        cost_estimate=pl.CostEstimate(
            flops=6 * requests * qlen * q_part * keys,
            bytes_accessed=4 * requests * qlen * q_part + 2 * requests * NPASS * 2 * PLEN * kv_width,
            transcendentals=requests * qlen * (q_part // HEAD_DIM) * keys,
        ),
    )(slot_index, *operands)


def here():
    store, head = lax.axis_index("store"), lax.axis_index("head")
    return store * 2 + head, (store * 2 + head) // PLANE, (store * 2 + head) % PLANE


def remote(src, dst, send_sem, recv_sem, peer):
    return pltpu.make_async_remote_copy(
        src_ref=src,
        dst_ref=dst,
        send_sem=send_sem,
        recv_sem=recv_sem,
        device_id={"store": peer // 2, "head": peer % 2},
        device_id_type=pl.DeviceIdType.MESH,
    )


def greet_all(me, count):
    barrier = pltpu.get_barrier_semaphore()

    def greet(k, carry):
        peer = (me + k) % count
        pl.semaphore_signal(
            barrier,
            inc=1,
            device_id={"store": peer // 2, "head": peer % 2},
            device_id_type=pl.DeviceIdType.MESH,
        )
        return carry

    lax.fori_loop(1, count, greet, 0)
    pl.semaphore_wait(barrier, count - 1)


def near_kernel(out_ref, kv_ref, in_ref, relay_ref, send, recv, keep):
    me, plane, spot = here()
    outer = (plane == 0) | (plane == 3)
    inner = (plane == 1) | (plane == 2)
    greet_all(me, 4 * PLANE)
    whole = remote(
        kv_ref, relay_ref, send.at[8], recv.at[8], jnp.where(plane == 0, 2, 1) * PLANE + spot
    )

    def block(k, target_plane):
        peer = target_plane * PLANE + (spot + k % PLANE) % PLANE
        return remote(out_ref.at[peer], in_ref.at[me], send.at[k], recv.at[k], peer)

    out_plane = jnp.where(plane == 1, 0, 3)

    @pl.when(outer)
    def _():
        whole.start()

    @pl.when(inner)
    def _():
        for k in range(PLANE):
            block(PLANE + k, out_plane).start()

    for k in range(1, PLANE):
        block(k, plane).start()
    own = pltpu.make_async_copy(out_ref.at[me], in_ref.at[me], keep)
    own.start()
    own.wait()
    for k in range(1, PLANE):
        block(k, plane).wait()

    @pl.when(outer)
    def _():
        for k in range(PLANE):
            block(PLANE + k, plane).wait_recv()
        whole.wait_send()

    @pl.when(inner)
    def _():
        for k in range(PLANE):
            block(PLANE + k, out_plane).wait_send()
        whole.wait_recv()


def far_kernel(out_ref, relay_ref, have_ref, in_ref, send, recv, keep):
    me, plane, spot = here()
    outer = (plane == 0) | (plane == 3)
    inner = (plane == 1) | (plane == 2)
    greet_all(me, 4 * PLANE)
    origin = jnp.where(plane == 2, 0, 3) * PLANE + spot

    def block(k, target_plane):
        peer = target_plane * PLANE + (spot + k % PLANE) % PLANE
        return remote(out_ref.at[peer], in_ref.at[me], send.at[k], recv.at[k], peer)

    def relayed(k, step, target_plane):
        spot_there = (spot + k % PLANE) % PLANE
        return remote(
            relay_ref.at[step, spot_there],
            in_ref.at[origin],
            send.at[k],
            recv.at[k],
            target_plane * PLANE + spot_there,
        )

    inward = jnp.where(plane == 0, 1, 2)
    across = jnp.where(plane == 1, 2, 1)
    beyond = jnp.where(plane == 1, 3, 0)
    out_plane = jnp.where(plane == 1, 0, 3)
    own = pltpu.make_async_copy(relay_ref.at[0, spot], in_ref.at[origin], keep)

    @pl.when(outer)
    def _():
        for k in range(PLANE):
            block(k, inward).start()
        for k in range(PLANE):
            block(k, inward).wait_send()
        for k in range(PLANE):
            block(2 * PLANE + k, inward).wait_recv()
            relayed(4 * PLANE + k, 1, inward).wait_recv()

    @pl.when(inner)
    def _():
        for k in range(PLANE):
            block(2 * PLANE + k, beyond).start()
            relayed(4 * PLANE + k, 1, out_plane).start()
            block(PLANE + k, across).start()
        for k in range(1, PLANE):
            relayed(3 * PLANE + k, 0, plane).start()
        own.start()
        own.wait()
        for k in range(PLANE):
            block(2 * PLANE + k, beyond).wait_send()
            relayed(4 * PLANE + k, 1, out_plane).wait_send()
            block(PLANE + k, across).wait()
            block(k, across).wait_recv()
        for k in range(1, PLANE):
            relayed(3 * PLANE + k, 0, plane).wait()


def tell_kernel(asked_ref, told_ref, send, recv):
    me, plane, spot = here()
    count = told_ref.shape[0]
    store, head = me // 2, me % 2
    barrier = pltpu.get_barrier_semaphore()

    def greet(k, carry):
        pl.semaphore_signal(
            barrier,
            inc=1,
            device_id={"store": (store + k) % count},
            device_id_type=pl.DeviceIdType.MESH,
        )
        return carry

    lax.fori_loop(1, count, greet, 0)
    told_ref[store] = asked_ref[...]
    pl.semaphore_wait(barrier, count - 1)

    def table(k):
        peer = (store + k) % count * 2 + head
        return remote(asked_ref, told_ref.at[store], send.at[k], recv.at[k], peer)

    for k in range(1, count):
        table(k).start()
    for k in range(1, count):
        table(k).wait()


def tell(asked, store_count):
    table = jnp.pad(asked, ((0, 0), (0, 128 - asked.shape[1])))
    told = pl.pallas_call(
        tell_kernel,
        out_shape=jax.ShapeDtypeStruct((store_count,) + table.shape, jnp.int32),
        in_specs=[pl.BlockSpec(memory_space=pltpu.VMEM)],
        out_specs=pl.BlockSpec(memory_space=pltpu.VMEM),
        scratch_shapes=[pltpu.SemaphoreType.DMA((store_count,))] * 2,
        compiler_params=pltpu.CompilerParams(collective_id=3, has_side_effects=True),
    )(table)
    return told[:, :, : asked.shape[1]]


def exchange(wanted_all, outgoing, passage_kv):
    any_space = pl.BlockSpec(memory_space=pl.ANY)
    incoming, relay = pl.pallas_call(
        near_kernel,
        out_shape=[
            jax.ShapeDtypeStruct(outgoing.shape, jnp.bfloat16),
            jax.ShapeDtypeStruct(passage_kv.shape, jnp.bfloat16),
        ],
        in_specs=[any_space] * 2,
        out_specs=[any_space] * 2,
        scratch_shapes=[
            pltpu.SemaphoreType.DMA((9,)),
            pltpu.SemaphoreType.DMA((9,)),
            pltpu.SemaphoreType.DMA,
        ],
        compiler_params=pltpu.CompilerParams(collective_id=1, has_side_effects=True, vmem_limit_bytes=VMEM_LIMIT),
    )(outgoing, passage_kv)
    me, plane, spot = here()
    origin = jnp.where(plane == 2, 0, 3) * PLANE + spot
    for_origin = lax.dynamic_index_in_dim(wanted_all, origin, 1, keepdims=False)
    cap = for_origin.shape[1]
    by_plane = for_origin.reshape(4, 2, cap)
    out_plane = jnp.where(plane == 1, 0, 3)
    lists = jnp.concatenate(
        [
            lax.dynamic_index_in_dim(by_plane, plane, 0, keepdims=False),
            lax.dynamic_index_in_dim(by_plane, out_plane, 0, keepdims=False),
        ],
        axis=0,
    )
    lists = jnp.repeat(lists, 2, axis=0)
    relay_out = pack(lists, relay, 4, 2, cap, 1)[0]
    relay_out = relay_out.reshape((2, PLANE) + relay_out.shape[1:])
    return pl.pallas_call(
        far_kernel,
        out_shape=jax.ShapeDtypeStruct(outgoing.shape, jnp.bfloat16),
        in_specs=[any_space] * 3,
        out_specs=any_space,
        input_output_aliases={2: 0},
        scratch_shapes=[
            pltpu.SemaphoreType.DMA((5 * PLANE,)),
            pltpu.SemaphoreType.DMA((5 * PLANE,)),
            pltpu.SemaphoreType.DMA,
        ],
        compiler_params=pltpu.CompilerParams(collective_id=2, has_side_effects=True, vmem_limit_bytes=VMEM_LIMIT),
    )(outgoing, relay_out, incoming)


def local(queries, own_keys, own_values, passage_kv, passage_rows, retrieval, offsets):
    stored_count = passage_kv.shape[0]
    store_count = lax.axis_size("store")
    head_count = lax.axis_size("head")
    peer_count = store_count * head_count
    requests = queries.shape[0]
    pick_ids = retrieval.reshape(-1)
    pick_count = pick_ids.shape[0]
    cap_dev = 3 * pick_count // (2 * peer_count)
    store_rows = passage_rows[pick_ids]
    owner_dev = store_rows // stored_count
    local_row = store_rows % stored_count
    slot_index = owner_dev * cap_dev + ranks_within(owner_dev)
    asked = request_table(slot_index, local_row, peer_count * cap_dev).reshape(peer_count, cap_dev)
    relays = store_count == 8 and head_count == 2 and 2 * cap_dev >= stored_count
    if relays:
        wanted_all = tell(asked, store_count)
        wanted = jnp.repeat(wanted_all[:, here()[0]], head_count, axis=0)
    else:
        wanted = lax.all_to_all(asked, ("store", "head"), split_axis=0, concat_axis=0, tiled=True)
    outgoing = pack(wanted, passage_kv, store_count, head_count, cap_dev, CHUNKS)

    turn_by = jnp.arange(pick_count, dtype=jnp.int32) % NPASS * PLEN - offsets[pick_ids]
    half_dim = HEAD_DIM // 2
    inverse_freq = rope_theta ** (-(jnp.arange(half_dim, dtype=jnp.float32) * 2.0) / HEAD_DIM)
    angles = turn_by.astype(jnp.float32)[:, None] * inverse_freq[None, :]
    cosine, sine = jnp.cos(angles), jnp.sin(angles)
    cosine = jnp.concatenate([cosine, cosine], axis=1).reshape(requests, NPASS, HEAD_DIM)
    sine = jnp.concatenate([-sine, sine], axis=1).reshape(requests, NPASS, HEAD_DIM)

    result = None
    for chunk in range(CHUNKS):
        if relays:
            incoming = exchange(wanted_all, outgoing[chunk], passage_kv)
        else:
            incoming = lax.all_to_all(
                outgoing[chunk], ("store", "head"), split_axis=0, concat_axis=0, tiled=True
            )
        fetched = incoming.reshape((peer_count * cap_dev,) + incoming.shape[2:])
        result = attend(
            chunk, CHUNKS, slot_index, queries, own_keys, own_values, cosine, sine, fetched, result
        )
    return result


def solution(mesh):
    in_specs = (
        P(("parts", "store"), None, "head"),
        P(("parts", "store"), None, "head"),
        P(("parts", "store"), None, "head"),
        P(("parts", "store", "head"), None, None, None),
        P("parts"),
        P(("parts", "store"), None),
        P("parts"),
    )
    out_specs = P(("parts", "store"), None, "head")
    return jax.shard_map(local, mesh=mesh, in_specs=in_specs, out_specs=out_specs, check_vma=False)
```

```python
import functools

import jax
import jax.numpy as jnp
from jax import lax
from jax.experimental import pallas as pl
from jax.experimental.pallas import tpu as pltpu
from jax.sharding import PartitionSpec as P

HEAD_DIM = 128
NPASS = 16
PLEN = 32
CHUNKS = 1
PLANE = 4
VMEM_LIMIT = 60 * 1024 * 1024
ROWS_AT_ONCE = 128

rope_theta = 1000000.0
EXP2_SCALE = HEAD_DIM ** (-0.5) * 1.4426950408889634


def ranks_within(owner_ids):
    count = owner_ids.shape[0]
    same_owner = owner_ids[:, None] == owner_ids[None, :]
    earlier = jnp.arange(count)[None, :] < jnp.arange(count)[:, None]
    return jnp.sum(same_owner & earlier, axis=1)


def request_table(slot_index, local_row, total):
    hits = slot_index[:, None] == jnp.arange(total)[None, :]
    return jnp.sum(jnp.where(hits, local_row[:, None], 0), axis=0)


def pack_kernel(store_count, head_count, cap, width, wanted_ref, kv_ref, *rest):
    outs, sems = rest[:-1], rest[-1]
    half = kv_ref.shape[3] // head_count
    for chunk, out_ref in enumerate(outs):
        for head in range(head_count):
            lanes = pl.ds(head * half + chunk * width, width)

            def one_slot(i, carry):
                peer = (i // cap) * head_count + head
                j = i % cap
                row = wanted_ref[peer * cap + j]
                pltpu.make_async_copy(
                    kv_ref.at[row, :, :, lanes], out_ref.at[peer, j], sems.at[chunk]
                ).start()
                return carry

            lax.fori_loop(0, store_count * cap, one_slot, 0)
    for chunk, out_ref in enumerate(outs):
        pltpu.make_async_copy(out_ref, out_ref, sems.at[chunk]).wait()


def pack(wanted, passage_kv, store_count, head_count, cap, chunks):
    width = passage_kv.shape[3] // head_count // chunks
    shape = jax.ShapeDtypeStruct((store_count * head_count, cap, 2, PLEN, width), jnp.bfloat16)
    return pl.pallas_call(
        functools.partial(pack_kernel, store_count, head_count, cap, width),
        out_shape=[shape] * chunks,
        in_specs=[
            pl.BlockSpec(memory_space=pltpu.SMEM),
            pl.BlockSpec(memory_space=pltpu.VMEM),
        ],
        out_specs=[pl.BlockSpec(memory_space=pl.ANY)] * chunks,
        scratch_shapes=[pltpu.SemaphoreType.DMA((chunks,))],
        compiler_params=pltpu.CompilerParams(vmem_limit_bytes=VMEM_LIMIT),
    )(wanted.reshape(-1), passage_kv)


def attend_kernel(group, slot_ref, q_ref, own_k_ref, own_v_ref, cos_ref, sin_ref, *rest):
    pages = rest[:NPASS]
    out_ref = rest[-1]
    qlen = q_ref.shape[1]
    kv_count = own_k_ref.shape[2] // HEAD_DIM
    span = ROWS_AT_ONCE // qlen
    ones = jnp.ones((NPASS * PLEN + qlen, HEAD_DIM), jnp.bfloat16)
    token = lax.broadcasted_iota(jnp.int32, (ROWS_AT_ONCE, qlen), 0) % qlen
    visible = lax.broadcasted_iota(jnp.int32, (ROWS_AT_ONCE, qlen), 1) <= token
    for kv in range(kv_count):
        lanes = slice(kv * HEAD_DIM, (kv + 1) * HEAD_DIM)
        keys = []
        for j in range(NPASS):
            stored = pages[j][0, 0, :, lanes].astype(jnp.float32)
            turned = stored * cos_ref[0, j : j + 1, :] + pltpu.roll(
                stored, HEAD_DIM // 2, 1
            ) * sin_ref[0, j : j + 1, :]
            keys.append(turned.astype(jnp.bfloat16))
        keys = jnp.concatenate(keys + [own_k_ref[0, :, lanes]], axis=0)
        values = jnp.concatenate(
            [pages[j][0, 1, :, lanes] for j in range(NPASS)] + [own_v_ref[0, :, lanes]], axis=0
        )
        values = jnp.concatenate([values, ones], axis=1)
        for first in range(0, group, span):
            heads = [kv * group + first + g for g in range(span)]
            question = jnp.concatenate(
                [q_ref[0, :, h * HEAD_DIM : (h + 1) * HEAD_DIM] for h in heads], axis=0
            )
            scores = lax.dot_general(
                question, keys, (((1,), (1,)), ((), ())), preferred_element_type=jnp.float32
            )
            own = jnp.where(visible, scores[:, NPASS * PLEN :], -jnp.inf)
            scores = jnp.concatenate([scores[:, : NPASS * PLEN], own], axis=1)
            peak = jnp.max(scores, axis=1, keepdims=True)
            expo = jnp.exp2((scores - peak) * EXP2_SCALE).astype(jnp.bfloat16)
            both = jnp.dot(expo, values, preferred_element_type=jnp.float32)
            result = (both[:, :HEAD_DIM] / both[:, HEAD_DIM:]).astype(jnp.bfloat16)
            for g, h in enumerate(heads):
                out_ref[0, :, h * HEAD_DIM : (h + 1) * HEAD_DIM] = result[g * qlen : (g + 1) * qlen]


def attend(chunk, chunks, slot_index, queries, own_keys, own_values, cosine, sine, fetched, so_far):
    requests, qlen, q_width = queries.shape
    kv_width = own_keys.shape[2] // chunks
    q_part = q_width // chunks
    group = q_part // kv_width
    page = fetched.shape[1:]

    def by_chunk(r, slots):
        return (r, 0, chunk)

    def by_request(r, slots):
        return (r, 0, 0)

    def page_spec(j):
        return pl.BlockSpec((1,) + page, lambda r, slots: (slots[r * NPASS + j], 0, 0, 0))

    in_specs = [
        pl.BlockSpec((1, qlen, q_part), by_chunk),
        pl.BlockSpec((1, qlen, kv_width), by_chunk),
        pl.BlockSpec((1, qlen, kv_width), by_chunk),
        pl.BlockSpec((1, NPASS, HEAD_DIM), by_request),
        pl.BlockSpec((1, NPASS, HEAD_DIM), by_request),
    ] + [page_spec(j) for j in range(NPASS)]
    operands = [queries, own_keys, own_values, cosine, sine] + [fetched] * NPASS
    aliases = {}
    if so_far is not None:
        in_specs.append(pl.BlockSpec(memory_space=pl.ANY))
        aliases = {1 + len(operands): 0}
        operands.append(so_far)
    keys = NPASS * PLEN + qlen
    return pl.pallas_call(
        functools.partial(attend_kernel, group),
        grid_spec=pltpu.PrefetchScalarGridSpec(
            num_scalar_prefetch=1,
            grid=(requests,),
            in_specs=in_specs,
            out_specs=pl.BlockSpec((1, qlen, q_part), by_chunk),
        ),
        out_shape=jax.ShapeDtypeStruct(queries.shape, jnp.bfloat16),
        input_output_aliases=aliases,
        compiler_params=pltpu.CompilerParams(vmem_limit_bytes=VMEM_LIMIT),
        cost_estimate=pl.CostEstimate(
            flops=6 * requests * qlen * q_part * keys,
            bytes_accessed=4 * requests * qlen * q_part + 2 * requests * NPASS * 2 * PLEN * kv_width,
            transcendentals=requests * qlen * (q_part // HEAD_DIM) * keys,
        ),
    )(slot_index, *operands)


def here():
    store, head = lax.axis_index("store"), lax.axis_index("head")
    return store * 2 + head, (store * 2 + head) // PLANE, (store * 2 + head) % PLANE


def remote(src, dst, send_sem, recv_sem, peer):
    return pltpu.make_async_remote_copy(
        src_ref=src,
        dst_ref=dst,
        send_sem=send_sem,
        recv_sem=recv_sem,
        device_id={"store": peer // 2, "head": peer % 2},
        device_id_type=pl.DeviceIdType.MESH,
    )


def greet_all(me, count):
    barrier = pltpu.get_barrier_semaphore()

    def greet(k, carry):
        peer = (me + k) % count
        pl.semaphore_signal(
            barrier,
            inc=1,
            device_id={"store": peer // 2, "head": peer % 2},
            device_id_type=pl.DeviceIdType.MESH,
        )
        return carry

    lax.fori_loop(1, count, greet, 0)
    pl.semaphore_wait(barrier, count - 1)


def exchange_kernel(lists_ref, out_ref, kv_ref, in_ref, store_buf, relay_buf, send, recv, keep):
    me, plane, spot = here()
    outer = (plane == 0) | (plane == 3)
    inner = (plane == 1) | (plane == 2)
    greet_all(me, 4 * PLANE)
    inward = jnp.where(plane == 0, 1, 2)
    across = jnp.where(plane == 1, 2, 1)
    beyond = jnp.where(plane == 1, 3, 0)
    out_plane = jnp.where(plane == 1, 0, 3)
    origin = jnp.where(plane == 2, 0, 3) * PLANE + spot
    cap = relay_buf.shape[2]
    half = relay_buf.shape[5]
    OWN, OUT, INWARD, ACROSS, BEYOND, RELAY_OWN, RELAY_OUT = range(0, 7 * PLANE, PLANE)
    whole_sem = 7 * PLANE
    whole = remote(
        kv_ref,
        store_buf,
        send.at[whole_sem],
        recv.at[whole_sem],
        jnp.where(plane == 0, 2, 1) * PLANE + spot,
    )

    def block(kind, k, target_plane):
        peer = target_plane * PLANE + (spot + k) % PLANE
        return remote(out_ref.at[peer], in_ref.at[me], send.at[kind + k], recv.at[kind + k], peer)

    def relayed(kind, k, step, target_plane):
        spot_there = (spot + k) % PLANE
        return remote(
            relay_buf.at[step, spot_there],
            in_ref.at[origin],
            send.at[kind + k],
            recv.at[kind + k],
            target_plane * PLANE + spot_there,
        )

    def fill(step, k):
        spot_there = (spot + k) % PLANE
        head = spot_there % 2

        for side in range(2):

            @pl.when(head == side)
            def _():
                def one_page(i, carry):
                    row = lists_ref[(step * PLANE + spot_there) * cap + i]
                    relay_buf[step, spot_there, i] = store_buf[
                        row, :, :, side * half : (side + 1) * half
                    ]
                    return carry

                lax.fori_loop(0, cap, one_page, 0)

    own = pltpu.make_async_copy(out_ref.at[me], in_ref.at[me], keep.at[0])
    own_relay = pltpu.make_async_copy(relay_buf.at[0, spot], in_ref.at[origin], keep.at[1])

    @pl.when(outer)
    def _():
        whole.start()

    @pl.when(inner)
    def _():
        for k in range(PLANE):
            block(BEYOND, k, beyond).start()
            block(OUT, k, out_plane).start()

    for k in range(1, PLANE):
        block(OWN, k, plane).start()
    own.start()

    @pl.when(outer)
    def _():
        whole.wait_send()
        for k in range(PLANE):
            block(INWARD, k, inward).start()
        for k in range(PLANE):
            block(INWARD, k, inward).wait_send()
        for k in range(PLANE):
            block(OUT, k, plane).wait_recv()
            block(BEYOND, k, plane).wait_recv()
            relayed(RELAY_OUT, k, 1, plane).wait_recv()

    @pl.when(inner)
    def _():
        whole.wait_recv()
        for k in range(PLANE):
            block(ACROSS, k, across).start()
        for k in range(PLANE):
            fill(1, k)
            relayed(RELAY_OUT, k, 1, out_plane).start()
        for k in range(1, PLANE):
            fill(0, k)
            relayed(RELAY_OWN, k, 0, plane).start()
        fill(0, 0)
        own_relay.start()
        own_relay.wait()
        for k in range(PLANE):
            block(BEYOND, k, beyond).wait_send()
            block(OUT, k, out_plane).wait_send()
            relayed(RELAY_OUT, k, 1, out_plane).wait_send()
            block(ACROSS, k, across).wait()
            block(INWARD, k, plane).wait_recv()
        for k in range(1, PLANE):
            relayed(RELAY_OWN, k, 0, plane).wait()

    own.wait()
    for k in range(1, PLANE):
        block(OWN, k, plane).wait()


def tell_kernel(asked_ref, told_ref, send, recv):
    me, plane, spot = here()
    count = told_ref.shape[0]
    store, head = me // 2, me % 2
    barrier = pltpu.get_barrier_semaphore()

    def greet(k, carry):
        pl.semaphore_signal(
            barrier,
            inc=1,
            device_id={"store": (store + k) % count},
            device_id_type=pl.DeviceIdType.MESH,
        )
        return carry

    lax.fori_loop(1, count, greet, 0)
    told_ref[store] = asked_ref[...]
    pl.semaphore_wait(barrier, count - 1)

    def table(k):
        peer = (store + k) % count * 2 + head
        return remote(asked_ref, told_ref.at[store], send.at[k], recv.at[k], peer)

    for k in range(1, count):
        table(k).start()
    for k in range(1, count):
        table(k).wait()


def tell(asked, store_count):
    table = jnp.pad(asked, ((0, 0), (0, 128 - asked.shape[1])))
    told = pl.pallas_call(
        tell_kernel,
        out_shape=jax.ShapeDtypeStruct((store_count,) + table.shape, jnp.int32),
        in_specs=[pl.BlockSpec(memory_space=pltpu.VMEM)],
        out_specs=pl.BlockSpec(memory_space=pltpu.VMEM),
        scratch_shapes=[pltpu.SemaphoreType.DMA((store_count,))] * 2,
        compiler_params=pltpu.CompilerParams(collective_id=3, has_side_effects=True),
    )(table)
    return told[:, :, : asked.shape[1]]


def exchange(wanted_all, outgoing, passage_kv):
    any_space = pl.BlockSpec(memory_space=pl.ANY)
    me, plane, spot = here()
    origin = jnp.where(plane == 2, 0, 3) * PLANE + spot
    for_origin = lax.dynamic_index_in_dim(wanted_all, origin, 1, keepdims=False)
    cap = for_origin.shape[1]
    by_plane = for_origin.reshape(4, 2, cap)
    out_plane = jnp.where(plane == 1, 0, 3)
    lists = jnp.concatenate(
        [
            lax.dynamic_index_in_dim(by_plane, plane, 0, keepdims=False),
            lax.dynamic_index_in_dim(by_plane, out_plane, 0, keepdims=False),
        ],
        axis=0,
    )
    lists = jnp.repeat(lists, 2, axis=0).reshape(-1)
    return pl.pallas_call(
        exchange_kernel,
        out_shape=jax.ShapeDtypeStruct(outgoing.shape, jnp.bfloat16),
        in_specs=[pl.BlockSpec(memory_space=pltpu.SMEM), any_space, any_space],
        out_specs=any_space,
        scratch_shapes=[
            pltpu.VMEM(passage_kv.shape, jnp.bfloat16),
            pltpu.VMEM((2, PLANE) + outgoing.shape[1:], jnp.bfloat16),
            pltpu.SemaphoreType.DMA((7 * PLANE + 1,)),
            pltpu.SemaphoreType.DMA((7 * PLANE + 1,)),
            pltpu.SemaphoreType.DMA((2,)),
        ],
        compiler_params=pltpu.CompilerParams(
            collective_id=1, has_side_effects=True, vmem_limit_bytes=VMEM_LIMIT
        ),
    )(lists, outgoing, passage_kv)


def local(queries, own_keys, own_values, passage_kv, passage_rows, retrieval, offsets):
    stored_count = passage_kv.shape[0]
    store_count = lax.axis_size("store")
    head_count = lax.axis_size("head")
    peer_count = store_count * head_count
    requests = queries.shape[0]
    pick_ids = retrieval.reshape(-1)
    pick_count = pick_ids.shape[0]
    cap_dev = 3 * pick_count // (2 * peer_count)
    store_rows = passage_rows[pick_ids]
    owner_dev = store_rows // stored_count
    local_row = store_rows % stored_count
    slot_index = owner_dev * cap_dev + ranks_within(owner_dev)
    asked = request_table(slot_index, local_row, peer_count * cap_dev).reshape(peer_count, cap_dev)
    relays = store_count == 8 and head_count == 2 and 2 * cap_dev >= stored_count
    if relays:
        wanted_all = tell(asked, store_count)
        wanted = jnp.repeat(wanted_all[:, here()[0]], head_count, axis=0)
    else:
        wanted = lax.all_to_all(asked, ("store", "head"), split_axis=0, concat_axis=0, tiled=True)
    outgoing = pack(wanted, passage_kv, store_count, head_count, cap_dev, CHUNKS)

    turn_by = jnp.arange(pick_count, dtype=jnp.int32) % NPASS * PLEN - offsets[pick_ids]
    half_dim = HEAD_DIM // 2
    inverse_freq = rope_theta ** (-(jnp.arange(half_dim, dtype=jnp.float32) * 2.0) / HEAD_DIM)
    angles = turn_by.astype(jnp.float32)[:, None] * inverse_freq[None, :]
    cosine, sine = jnp.cos(angles), jnp.sin(angles)
    cosine = jnp.concatenate([cosine, cosine], axis=1).reshape(requests, NPASS, HEAD_DIM)
    sine = jnp.concatenate([-sine, sine], axis=1).reshape(requests, NPASS, HEAD_DIM)

    result = None
    for chunk in range(CHUNKS):
        if relays:
            incoming = exchange(wanted_all, outgoing[chunk], passage_kv)
        else:
            incoming = lax.all_to_all(
                outgoing[chunk], ("store", "head"), split_axis=0, concat_axis=0, tiled=True
            )
        fetched = incoming.reshape((peer_count * cap_dev,) + incoming.shape[2:])
        result = attend(
            chunk, CHUNKS, slot_index, queries, own_keys, own_values, cosine, sine, fetched, result
        )
    return result


def solution(mesh):
    in_specs = (
        P(("parts", "store"), None, "head"),
        P(("parts", "store"), None, "head"),
        P(("parts", "store"), None, "head"),
        P(("parts", "store", "head"), None, None, None),
        P("parts"),
        P(("parts", "store"), None),
        P("parts"),
    )
    out_specs = P(("parts", "store"), None, "head")
    return jax.shard_map(local, mesh=mesh, in_specs=in_specs, out_specs=out_specs, check_vma=False)
```

```python
import functools

import jax
import jax.numpy as jnp
from jax import lax
from jax.experimental import pallas as pl
from jax.experimental.pallas import tpu as pltpu
from jax.sharding import PartitionSpec as P

HEAD_DIM = 128
NPASS = 16
PLEN = 32
CHUNKS = 1
PLANE = 4
VMEM_LIMIT = 60 * 1024 * 1024
ROWS_AT_ONCE = 128

rope_theta = 1000000.0
EXP2_SCALE = HEAD_DIM ** (-0.5) * 1.4426950408889634


def ranks_within(owner_ids):
    count = owner_ids.shape[0]
    same_owner = owner_ids[:, None] == owner_ids[None, :]
    earlier = jnp.arange(count)[None, :] < jnp.arange(count)[:, None]
    return jnp.sum(same_owner & earlier, axis=1)


def request_table(slot_index, local_row, total):
    hits = slot_index[:, None] == jnp.arange(total)[None, :]
    return jnp.sum(jnp.where(hits, local_row[:, None], 0), axis=0)


def pack_kernel(store_count, head_count, cap, width, wanted_ref, kv_ref, *rest):
    outs, sems = rest[:-1], rest[-1]
    half = kv_ref.shape[3] // head_count
    for chunk, out_ref in enumerate(outs):
        for head in range(head_count):
            lanes = pl.ds(head * half + chunk * width, width)

            def one_slot(i, carry):
                peer = (i // cap) * head_count + head
                j = i % cap
                row = wanted_ref[peer * cap + j]
                pltpu.make_async_copy(
                    kv_ref.at[row, :, :, lanes], out_ref.at[peer, j], sems.at[chunk]
                ).start()
                return carry

            lax.fori_loop(0, store_count * cap, one_slot, 0)
    for chunk, out_ref in enumerate(outs):
        pltpu.make_async_copy(out_ref, out_ref, sems.at[chunk]).wait()


def pack(wanted, passage_kv, store_count, head_count, cap, chunks):
    width = passage_kv.shape[3] // head_count // chunks
    shape = jax.ShapeDtypeStruct((store_count * head_count, cap, 2, PLEN, width), jnp.bfloat16)
    return pl.pallas_call(
        functools.partial(pack_kernel, store_count, head_count, cap, width),
        out_shape=[shape] * chunks,
        in_specs=[
            pl.BlockSpec(memory_space=pltpu.SMEM),
            pl.BlockSpec(memory_space=pltpu.VMEM),
        ],
        out_specs=[pl.BlockSpec(memory_space=pl.ANY)] * chunks,
        scratch_shapes=[pltpu.SemaphoreType.DMA((chunks,))],
        compiler_params=pltpu.CompilerParams(vmem_limit_bytes=VMEM_LIMIT),
    )(wanted.reshape(-1), passage_kv)


def attend_kernel(group, slot_ref, q_ref, own_k_ref, own_v_ref, cos_ref, sin_ref, *rest):
    pages = rest[:NPASS]
    out_ref = rest[-1]
    qlen = q_ref.shape[1]
    kv_count = own_k_ref.shape[2] // HEAD_DIM
    span = ROWS_AT_ONCE // qlen
    ones = jnp.ones((NPASS * PLEN + qlen, HEAD_DIM), jnp.bfloat16)
    token = lax.broadcasted_iota(jnp.int32, (ROWS_AT_ONCE, qlen), 0) % qlen
    visible = lax.broadcasted_iota(jnp.int32, (ROWS_AT_ONCE, qlen), 1) <= token
    for kv in range(kv_count):
        lanes = slice(kv * HEAD_DIM, (kv + 1) * HEAD_DIM)
        keys = []
        for j in range(NPASS):
            stored = pages[j][0, 0, :, lanes].astype(jnp.float32)
            turned = stored * cos_ref[0, j : j + 1, :] + pltpu.roll(
                stored, HEAD_DIM // 2, 1
            ) * sin_ref[0, j : j + 1, :]
            keys.append(turned.astype(jnp.bfloat16))
        keys = jnp.concatenate(keys + [own_k_ref[0, :, lanes]], axis=0)
        values = jnp.concatenate(
            [pages[j][0, 1, :, lanes] for j in range(NPASS)] + [own_v_ref[0, :, lanes]], axis=0
        )
        values = jnp.concatenate([values, ones], axis=1)
        for first in range(0, group, span):
            heads = [kv * group + first + g for g in range(span)]
            question = jnp.concatenate(
                [q_ref[0, :, h * HEAD_DIM : (h + 1) * HEAD_DIM] for h in heads], axis=0
            )
            scores = lax.dot_general(
                question, keys, (((1,), (1,)), ((), ())), preferred_element_type=jnp.float32
            )
            own = jnp.where(visible, scores[:, NPASS * PLEN :], -jnp.inf)
            scores = jnp.concatenate([scores[:, : NPASS * PLEN], own], axis=1)
            peak = jnp.max(scores, axis=1, keepdims=True)
            expo = jnp.exp2((scores - peak) * EXP2_SCALE).astype(jnp.bfloat16)
            both = jnp.dot(expo, values, preferred_element_type=jnp.float32)
            result = (both[:, :HEAD_DIM] / both[:, HEAD_DIM:]).astype(jnp.bfloat16)
            for g, h in enumerate(heads):
                out_ref[0, :, h * HEAD_DIM : (h + 1) * HEAD_DIM] = result[g * qlen : (g + 1) * qlen]


def attend(chunk, chunks, slot_index, queries, own_keys, own_values, cosine, sine, fetched, so_far):
    requests, qlen, q_width = queries.shape
    kv_width = own_keys.shape[2] // chunks
    q_part = q_width // chunks
    group = q_part // kv_width
    page = fetched.shape[1:]

    def by_chunk(r, slots):
        return (r, 0, chunk)

    def by_request(r, slots):
        return (r, 0, 0)

    def page_spec(j):
        return pl.BlockSpec((1,) + page, lambda r, slots: (slots[r * NPASS + j], 0, 0, 0))

    in_specs = [
        pl.BlockSpec((1, qlen, q_part), by_chunk),
        pl.BlockSpec((1, qlen, kv_width), by_chunk),
        pl.BlockSpec((1, qlen, kv_width), by_chunk),
        pl.BlockSpec((1, NPASS, HEAD_DIM), by_request),
        pl.BlockSpec((1, NPASS, HEAD_DIM), by_request),
    ] + [page_spec(j) for j in range(NPASS)]
    operands = [queries, own_keys, own_values, cosine, sine] + [fetched] * NPASS
    aliases = {}
    if so_far is not None:
        in_specs.append(pl.BlockSpec(memory_space=pl.ANY))
        aliases = {1 + len(operands): 0}
        operands.append(so_far)
    keys = NPASS * PLEN + qlen
    return pl.pallas_call(
        functools.partial(attend_kernel, group),
        grid_spec=pltpu.PrefetchScalarGridSpec(
            num_scalar_prefetch=1,
            grid=(requests,),
            in_specs=in_specs,
            out_specs=pl.BlockSpec((1, qlen, q_part), by_chunk),
        ),
        out_shape=jax.ShapeDtypeStruct(queries.shape, jnp.bfloat16),
        input_output_aliases=aliases,
        compiler_params=pltpu.CompilerParams(vmem_limit_bytes=VMEM_LIMIT),
        cost_estimate=pl.CostEstimate(
            flops=6 * requests * qlen * q_part * keys,
            bytes_accessed=4 * requests * qlen * q_part + 2 * requests * NPASS * 2 * PLEN * kv_width,
            transcendentals=requests * qlen * (q_part // HEAD_DIM) * keys,
        ),
    )(slot_index, *operands)


def here():
    store, head = lax.axis_index("store"), lax.axis_index("head")
    return store * 2 + head, (store * 2 + head) // PLANE, (store * 2 + head) % PLANE


def remote(src, dst, send_sem, recv_sem, peer):
    return pltpu.make_async_remote_copy(
        src_ref=src,
        dst_ref=dst,
        send_sem=send_sem,
        recv_sem=recv_sem,
        device_id={"store": peer // 2, "head": peer % 2},
        device_id_type=pl.DeviceIdType.MESH,
    )


def greet_all(me, count):
    barrier = pltpu.get_barrier_semaphore()

    def greet(k, carry):
        peer = (me + k) % count
        pl.semaphore_signal(
            barrier,
            inc=1,
            device_id={"store": peer // 2, "head": peer % 2},
            device_id_type=pl.DeviceIdType.MESH,
        )
        return carry

    lax.fori_loop(1, count, greet, 0)
    pl.semaphore_wait(barrier, count - 1)


def exchange_kernel(
    lists_ref, kv_ref, in_ref, mine_buf, out_ref, store_buf, relay_buf, send, recv, keep
):
    me, plane, spot = here()
    mine = pltpu.make_async_copy(kv_ref, mine_buf, keep.at[2])
    mine.start()
    outer = (plane == 0) | (plane == 3)
    inner = (plane == 1) | (plane == 2)
    greet_all(me, 4 * PLANE)
    inward = jnp.where(plane == 0, 1, 2)
    across = jnp.where(plane == 1, 2, 1)
    beyond = jnp.where(plane == 1, 3, 0)
    out_plane = jnp.where(plane == 1, 0, 3)
    origin = jnp.where(plane == 2, 0, 3) * PLANE + spot
    cap = relay_buf.shape[2]
    half = relay_buf.shape[5]
    OWN, OUT, INWARD, ACROSS, BEYOND, RELAY_OWN, RELAY_OUT = range(0, 7 * PLANE, PLANE)
    whole_sem = 7 * PLANE
    whole = remote(
        kv_ref,
        store_buf,
        send.at[whole_sem],
        recv.at[whole_sem],
        jnp.where(plane == 0, 2, 1) * PLANE + spot,
    )

    def block(kind, k, target_plane):
        peer = target_plane * PLANE + (spot + k) % PLANE
        return remote(out_ref.at[peer], in_ref.at[me], send.at[kind + k], recv.at[kind + k], peer)

    def relayed(kind, k, step, target_plane):
        spot_there = (spot + k) % PLANE
        return remote(
            relay_buf.at[step, spot_there],
            in_ref.at[origin],
            send.at[kind + k],
            recv.at[kind + k],
            target_plane * PLANE + spot_there,
        )

    def fill(source, target, first, head):
        for side in range(2):

            @pl.when(head == side)
            def _():
                def one_page(i, carry):
                    row = lists_ref[first + i]
                    target[i] = source[row, :, :, side * half : (side + 1) * half]
                    return carry

                lax.fori_loop(0, cap, one_page, 0)

    def fill_own(k, target_plane):
        peer = target_plane * PLANE + (spot + k) % PLANE
        fill(mine_buf, out_ref.at[peer], peer * cap, peer % 2)

    def fill_relay(step, k):
        spot_there = (spot + k) % PLANE
        first = (4 * PLANE + step * PLANE + spot_there) * cap
        fill(store_buf, relay_buf.at[step, spot_there], first, spot_there % 2)

    own = pltpu.make_async_copy(out_ref.at[me], in_ref.at[me], keep.at[0])
    own_relay = pltpu.make_async_copy(relay_buf.at[0, spot], in_ref.at[origin], keep.at[1])

    @pl.when(outer)
    def _():
        whole.start()

    mine.wait()

    @pl.when(inner)
    def _():
        for k in range(PLANE):
            fill_own(k, out_plane)
            block(OUT, k, out_plane).start()
            fill_own(k, beyond)
            block(BEYOND, k, beyond).start()

    for k in range(1, PLANE):
        fill_own(k, plane)
        block(OWN, k, plane).start()
    fill_own(0, plane)
    own.start()

    @pl.when(outer)
    def _():
        for k in range(PLANE):
            fill_own(k, inward)
        whole.wait_send()
        for k in range(PLANE):
            block(INWARD, k, inward).start()
        for k in range(PLANE):
            block(INWARD, k, inward).wait_send()
        for k in range(PLANE):
            block(OUT, k, plane).wait_recv()
            block(BEYOND, k, plane).wait_recv()
            relayed(RELAY_OUT, k, 1, plane).wait_recv()

    @pl.when(inner)
    def _():
        for k in range(PLANE):
            fill_own(k, across)
        whole.wait_recv()
        for k in range(PLANE):
            block(ACROSS, k, across).start()
        for k in range(PLANE):
            fill_relay(1, k)
            relayed(RELAY_OUT, k, 1, out_plane).start()
        for k in range(1, PLANE):
            fill_relay(0, k)
            relayed(RELAY_OWN, k, 0, plane).start()
        fill_relay(0, 0)
        own_relay.start()
        own_relay.wait()
        for k in range(PLANE):
            block(BEYOND, k, beyond).wait_send()
            block(OUT, k, out_plane).wait_send()
            relayed(RELAY_OUT, k, 1, out_plane).wait_send()
            block(ACROSS, k, across).wait()
            block(INWARD, k, plane).wait_recv()
        for k in range(1, PLANE):
            relayed(RELAY_OWN, k, 0, plane).wait()

    own.wait()
    for k in range(1, PLANE):
        block(OWN, k, plane).wait()


def tell_kernel(asked_ref, told_ref, send, recv):
    me, plane, spot = here()
    count = told_ref.shape[0]
    store, head = me // 2, me % 2
    barrier = pltpu.get_barrier_semaphore()

    def greet(k, carry):
        pl.semaphore_signal(
            barrier,
            inc=1,
            device_id={"store": (store + k) % count},
            device_id_type=pl.DeviceIdType.MESH,
        )
        return carry

    lax.fori_loop(1, count, greet, 0)
    told_ref[store] = asked_ref[...]
    pl.semaphore_wait(barrier, count - 1)

    def table(k):
        peer = (store + k) % count * 2 + head
        return remote(asked_ref, told_ref.at[store], send.at[k], recv.at[k], peer)

    for k in range(1, count):
        table(k).start()
    for k in range(1, count):
        table(k).wait()


def tell(asked, store_count):
    table = jnp.pad(asked, ((0, 0), (0, 128 - asked.shape[1])))
    told = pl.pallas_call(
        tell_kernel,
        out_shape=jax.ShapeDtypeStruct((store_count,) + table.shape, jnp.int32),
        in_specs=[pl.BlockSpec(memory_space=pltpu.VMEM)],
        out_specs=pl.BlockSpec(memory_space=pltpu.VMEM),
        scratch_shapes=[pltpu.SemaphoreType.DMA((store_count,))] * 2,
        compiler_params=pltpu.CompilerParams(collective_id=3, has_side_effects=True),
    )(table)
    return told[:, :, : asked.shape[1]]


def exchange(wanted_all, passage_kv):
    any_space = pl.BlockSpec(memory_space=pl.ANY)
    me, plane, spot = here()
    origin = jnp.where(plane == 2, 0, 3) * PLANE + spot
    for_origin = lax.dynamic_index_in_dim(wanted_all, origin, 1, keepdims=False)
    cap = for_origin.shape[1]
    by_plane = for_origin.reshape(4, 2, cap)
    out_plane = jnp.where(plane == 1, 0, 3)
    lists = jnp.concatenate(
        [
            lax.dynamic_index_in_dim(by_plane, plane, 0, keepdims=False),
            lax.dynamic_index_in_dim(by_plane, out_plane, 0, keepdims=False),
        ],
        axis=0,
    )
    lists = jnp.concatenate([wanted_all[:, me], lists], axis=0)
    lists = jnp.repeat(lists, 2, axis=0).reshape(-1)
    blocks = (4 * PLANE, cap, 2, PLEN, passage_kv.shape[3] // 2)
    return pl.pallas_call(
        exchange_kernel,
        out_shape=jax.ShapeDtypeStruct(blocks, jnp.bfloat16),
        in_specs=[pl.BlockSpec(memory_space=pltpu.SMEM), any_space],
        out_specs=any_space,
        scratch_shapes=[
            pltpu.VMEM(passage_kv.shape, jnp.bfloat16),
            pltpu.VMEM(blocks, jnp.bfloat16),
            pltpu.VMEM(passage_kv.shape, jnp.bfloat16),
            pltpu.VMEM((2, PLANE) + blocks[1:], jnp.bfloat16),
            pltpu.SemaphoreType.DMA((7 * PLANE + 1,)),
            pltpu.SemaphoreType.DMA((7 * PLANE + 1,)),
            pltpu.SemaphoreType.DMA((3,)),
        ],
        compiler_params=pltpu.CompilerParams(
            collective_id=1, has_side_effects=True, vmem_limit_bytes=VMEM_LIMIT
        ),
    )(lists, passage_kv)


def local(queries, own_keys, own_values, passage_kv, passage_rows, retrieval, offsets):
    stored_count = passage_kv.shape[0]
    store_count = lax.axis_size("store")
    head_count = lax.axis_size("head")
    peer_count = store_count * head_count
    requests = queries.shape[0]
    pick_ids = retrieval.reshape(-1)
    pick_count = pick_ids.shape[0]
    cap_dev = 3 * pick_count // (2 * peer_count)
    store_rows = passage_rows[pick_ids]
    owner_dev = store_rows // stored_count
    local_row = store_rows % stored_count
    slot_index = owner_dev * cap_dev + ranks_within(owner_dev)
    asked = request_table(slot_index, local_row, peer_count * cap_dev).reshape(peer_count, cap_dev)
    relays = store_count == 8 and head_count == 2 and 2 * cap_dev >= stored_count
    if relays:
        wanted_all = tell(asked, store_count)
    else:
        wanted = lax.all_to_all(asked, ("store", "head"), split_axis=0, concat_axis=0, tiled=True)
        outgoing = pack(wanted, passage_kv, store_count, head_count, cap_dev, CHUNKS)

    turn_by = jnp.arange(pick_count, dtype=jnp.int32) % NPASS * PLEN - offsets[pick_ids]
    half_dim = HEAD_DIM // 2
    inverse_freq = rope_theta ** (-(jnp.arange(half_dim, dtype=jnp.float32) * 2.0) / HEAD_DIM)
    angles = turn_by.astype(jnp.float32)[:, None] * inverse_freq[None, :]
    cosine, sine = jnp.cos(angles), jnp.sin(angles)
    cosine = jnp.concatenate([cosine, cosine], axis=1).reshape(requests, NPASS, HEAD_DIM)
    sine = jnp.concatenate([-sine, sine], axis=1).reshape(requests, NPASS, HEAD_DIM)

    result = None
    for chunk in range(CHUNKS):
        if relays:
            incoming = exchange(wanted_all, passage_kv)
        else:
            incoming = lax.all_to_all(
                outgoing[chunk], ("store", "head"), split_axis=0, concat_axis=0, tiled=True
            )
        fetched = incoming.reshape((peer_count * cap_dev,) + incoming.shape[2:])
        result = attend(
            chunk, CHUNKS, slot_index, queries, own_keys, own_values, cosine, sine, fetched, result
        )
    return result


def solution(mesh):
    in_specs = (
        P(("parts", "store"), None, "head"),
        P(("parts", "store"), None, "head"),
        P(("parts", "store"), None, "head"),
        P(("parts", "store", "head"), None, None, None),
        P("parts"),
        P(("parts", "store"), None),
        P("parts"),
    )
    out_specs = P(("parts", "store"), None, "head")
    return jax.shard_map(local, mesh=mesh, in_specs=in_specs, out_specs=out_specs, check_vma=False)
```

```python
import functools

import jax
import jax.numpy as jnp
from jax import lax
from jax.experimental import pallas as pl
from jax.experimental.pallas import tpu as pltpu
from jax.sharding import PartitionSpec as P

HEAD_DIM = 128
NPASS = 16
PLEN = 32
CHUNKS = 1
PLANE = 4
VMEM_LIMIT = 60 * 1024 * 1024
ROWS_AT_ONCE = 128

rope_theta = 1000000.0
EXP2_SCALE = HEAD_DIM ** (-0.5) * 1.4426950408889634


def ranks_within(owner_ids):
    count = owner_ids.shape[0]
    same_owner = owner_ids[:, None] == owner_ids[None, :]
    earlier = jnp.arange(count)[None, :] < jnp.arange(count)[:, None]
    return jnp.sum(same_owner & earlier, axis=1)


def request_table(slot_index, local_row, total):
    hits = slot_index[:, None] == jnp.arange(total)[None, :]
    return jnp.sum(jnp.where(hits, local_row[:, None], 0), axis=0)


def pack_kernel(store_count, head_count, cap, width, wanted_ref, kv_ref, *rest):
    outs, sems = rest[:-1], rest[-1]
    half = kv_ref.shape[3] // head_count
    for chunk, out_ref in enumerate(outs):
        for head in range(head_count):
            lanes = pl.ds(head * half + chunk * width, width)

            def one_slot(i, carry):
                peer = (i // cap) * head_count + head
                j = i % cap
                row = wanted_ref[peer * cap + j]
                pltpu.make_async_copy(
                    kv_ref.at[row, :, :, lanes], out_ref.at[peer, j], sems.at[chunk]
                ).start()
                return carry

            lax.fori_loop(0, store_count * cap, one_slot, 0)
    for chunk, out_ref in enumerate(outs):
        pltpu.make_async_copy(out_ref, out_ref, sems.at[chunk]).wait()


def pack(wanted, passage_kv, store_count, head_count, cap, chunks):
    width = passage_kv.shape[3] // head_count // chunks
    shape = jax.ShapeDtypeStruct((store_count * head_count, cap, 2, PLEN, width), jnp.bfloat16)
    return pl.pallas_call(
        functools.partial(pack_kernel, store_count, head_count, cap, width),
        out_shape=[shape] * chunks,
        in_specs=[
            pl.BlockSpec(memory_space=pltpu.SMEM),
            pl.BlockSpec(memory_space=pltpu.VMEM),
        ],
        out_specs=[pl.BlockSpec(memory_space=pl.ANY)] * chunks,
        scratch_shapes=[pltpu.SemaphoreType.DMA((chunks,))],
        compiler_params=pltpu.CompilerParams(vmem_limit_bytes=VMEM_LIMIT),
    )(wanted.reshape(-1), passage_kv)


def attend_kernel(group, slot_ref, q_ref, own_k_ref, own_v_ref, cos_ref, sin_ref, *rest):
    pages = rest[:NPASS]
    out_ref = rest[-1]
    qlen = q_ref.shape[1]
    kv_count = own_k_ref.shape[2] // HEAD_DIM
    span = ROWS_AT_ONCE // qlen
    ones = jnp.ones((NPASS * PLEN + qlen, HEAD_DIM), jnp.bfloat16)
    token = lax.broadcasted_iota(jnp.int32, (ROWS_AT_ONCE, qlen), 0) % qlen
    visible = lax.broadcasted_iota(jnp.int32, (ROWS_AT_ONCE, qlen), 1) <= token
    for kv in range(kv_count):
        lanes = slice(kv * HEAD_DIM, (kv + 1) * HEAD_DIM)
        keys = []
        for j in range(NPASS):
            stored = pages[j][0, 0, :, lanes].astype(jnp.float32)
            turned = stored * cos_ref[0, j : j + 1, :] + pltpu.roll(
                stored, HEAD_DIM // 2, 1
            ) * sin_ref[0, j : j + 1, :]
            keys.append(turned.astype(jnp.bfloat16))
        keys = jnp.concatenate(keys + [own_k_ref[0, :, lanes]], axis=0)
        values = jnp.concatenate(
            [pages[j][0, 1, :, lanes] for j in range(NPASS)] + [own_v_ref[0, :, lanes]], axis=0
        )
        values = jnp.concatenate([values, ones], axis=1)
        for first in range(0, group, span):
            heads = [kv * group + first + g for g in range(span)]
            question = jnp.concatenate(
                [q_ref[0, :, h * HEAD_DIM : (h + 1) * HEAD_DIM] for h in heads], axis=0
            )
            scores = lax.dot_general(
                question, keys, (((1,), (1,)), ((), ())), preferred_element_type=jnp.float32
            )
            own = jnp.where(visible, scores[:, NPASS * PLEN :], -jnp.inf)
            scores = jnp.concatenate([scores[:, : NPASS * PLEN], own], axis=1)
            peak = jnp.max(scores, axis=1, keepdims=True)
            expo = jnp.exp2((scores - peak) * EXP2_SCALE).astype(jnp.bfloat16)
            both = jnp.dot(expo, values, preferred_element_type=jnp.float32)
            result = (both[:, :HEAD_DIM] / both[:, HEAD_DIM:]).astype(jnp.bfloat16)
            for g, h in enumerate(heads):
                out_ref[0, :, h * HEAD_DIM : (h + 1) * HEAD_DIM] = result[g * qlen : (g + 1) * qlen]


def attend(chunk, chunks, slot_index, queries, own_keys, own_values, cosine, sine, fetched, so_far):
    requests, qlen, q_width = queries.shape
    kv_width = own_keys.shape[2] // chunks
    q_part = q_width // chunks
    group = q_part // kv_width
    page = fetched.shape[1:]

    def by_chunk(r, slots):
        return (r, 0, chunk)

    def by_request(r, slots):
        return (r, 0, 0)

    def page_spec(j):
        return pl.BlockSpec((1,) + page, lambda r, slots: (slots[r * NPASS + j], 0, 0, 0))

    in_specs = [
        pl.BlockSpec((1, qlen, q_part), by_chunk),
        pl.BlockSpec((1, qlen, kv_width), by_chunk),
        pl.BlockSpec((1, qlen, kv_width), by_chunk),
        pl.BlockSpec((1, NPASS, HEAD_DIM), by_request),
        pl.BlockSpec((1, NPASS, HEAD_DIM), by_request),
    ] + [page_spec(j) for j in range(NPASS)]
    operands = [queries, own_keys, own_values, cosine, sine] + [fetched] * NPASS
    aliases = {}
    if so_far is not None:
        in_specs.append(pl.BlockSpec(memory_space=pl.ANY))
        aliases = {1 + len(operands): 0}
        operands.append(so_far)
    keys = NPASS * PLEN + qlen
    return pl.pallas_call(
        functools.partial(attend_kernel, group),
        grid_spec=pltpu.PrefetchScalarGridSpec(
            num_scalar_prefetch=1,
            grid=(requests,),
            in_specs=in_specs,
            out_specs=pl.BlockSpec((1, qlen, q_part), by_chunk),
        ),
        out_shape=jax.ShapeDtypeStruct(queries.shape, jnp.bfloat16),
        input_output_aliases=aliases,
        compiler_params=pltpu.CompilerParams(vmem_limit_bytes=VMEM_LIMIT),
        cost_estimate=pl.CostEstimate(
            flops=6 * requests * qlen * q_part * keys,
            bytes_accessed=4 * requests * qlen * q_part + 2 * requests * NPASS * 2 * PLEN * kv_width,
            transcendentals=requests * qlen * (q_part // HEAD_DIM) * keys,
        ),
    )(slot_index, *operands)


def here():
    store, head = lax.axis_index("store"), lax.axis_index("head")
    return store * 2 + head, (store * 2 + head) // PLANE, (store * 2 + head) % PLANE


def remote(src, dst, send_sem, recv_sem, peer):
    return pltpu.make_async_remote_copy(
        src_ref=src,
        dst_ref=dst,
        send_sem=send_sem,
        recv_sem=recv_sem,
        device_id={"store": peer // 2, "head": peer % 2},
        device_id_type=pl.DeviceIdType.MESH,
    )


def greet_all(me, count):
    barrier = pltpu.get_barrier_semaphore()

    def greet(k, carry):
        peer = (me + k) % count
        pl.semaphore_signal(
            barrier,
            inc=1,
            device_id={"store": peer // 2, "head": peer % 2},
            device_id_type=pl.DeviceIdType.MESH,
        )
        return carry

    lax.fori_loop(1, count, greet, 0)
    pl.semaphore_wait(barrier, count - 1)


def exchange_kernel(
    lists_ref, kv_ref, in_ref, mine_buf, out_ref, store_buf, relay_buf, send, recv, keep
):
    me, plane, spot = here()
    mine = pltpu.make_async_copy(kv_ref, mine_buf, keep.at[2])
    mine.start()
    outer = (plane == 0) | (plane == 3)
    inner = (plane == 1) | (plane == 2)
    greet_all(me, 4 * PLANE)
    inward = jnp.where(plane == 0, 1, 2)
    across = jnp.where(plane == 1, 2, 1)
    beyond = jnp.where(plane == 1, 3, 0)
    out_plane = jnp.where(plane == 1, 0, 3)
    origin = jnp.where(plane == 2, 0, 3) * PLANE + spot
    cap = relay_buf.shape[2]
    half = relay_buf.shape[5]
    OWN, OUT, INWARD, ACROSS, BEYOND, RELAY_OWN, RELAY_OUT = range(0, 7 * PLANE, PLANE)
    whole_sem = 7 * PLANE
    whole = remote(
        kv_ref,
        store_buf,
        send.at[whole_sem],
        recv.at[whole_sem],
        jnp.where(plane == 0, 2, 1) * PLANE + spot,
    )

    def block(kind, k, target_plane):
        peer = target_plane * PLANE + (spot + k) % PLANE
        return remote(out_ref.at[peer], in_ref.at[me], send.at[kind + k], recv.at[kind + k], peer)

    def relayed(kind, k, step, target_plane):
        spot_there = (spot + k) % PLANE
        return remote(
            relay_buf.at[step, spot_there],
            in_ref.at[origin],
            send.at[kind + k],
            recv.at[kind + k],
            target_plane * PLANE + spot_there,
        )

    def fill(source, target, first, head):
        for side in range(2):

            @pl.when(head == side)
            def _():
                def one_page(i, carry):
                    row = lists_ref[first + i]
                    target[i] = source[row, :, :, side * half : (side + 1) * half]
                    return carry

                lax.fori_loop(0, cap, one_page, 0)

    def fill_own(k, target_plane):
        peer = target_plane * PLANE + (spot + k) % PLANE
        fill(mine_buf, out_ref.at[peer], peer * cap, peer % 2)

    def fill_relay(step, k):
        spot_there = (spot + k) % PLANE
        first = (4 * PLANE + step * PLANE + spot_there) * cap
        fill(store_buf, relay_buf.at[step, spot_there], first, spot_there % 2)

    own = pltpu.make_async_copy(out_ref.at[me], in_ref.at[me], keep.at[0])
    own_relay = pltpu.make_async_copy(relay_buf.at[0, spot], in_ref.at[origin], keep.at[1])

    @pl.when(outer)
    def _():
        whole.start()

    mine.wait()

    @pl.when(inner)
    def _():
        for k in range(PLANE):
            fill_own(k, out_plane)
            block(OUT, k, out_plane).start()
            fill_own(k, beyond)
            if k < PLANE // 2:
                block(BEYOND, k, beyond).start()

    for k in range(1, PLANE):
        fill_own(k, plane)
        block(OWN, k, plane).start()
    fill_own(0, plane)
    own.start()

    @pl.when(outer)
    def _():
        for k in range(PLANE):
            fill_own(k, inward)
        whole.wait_send()
        for k in range(PLANE):
            block(INWARD, k, inward).start()
        for k in range(PLANE):
            block(INWARD, k, inward).wait_send()
        for k in range(PLANE):
            block(OUT, k, plane).wait_recv()
            block(BEYOND, k, plane).wait_recv()
            relayed(RELAY_OUT, k, 1, plane).wait_recv()

    @pl.when(inner)
    def _():
        for k in range(PLANE):
            fill_own(k, across)
        whole.wait_recv()
        for k in range(PLANE // 2, PLANE):
            block(BEYOND, k, beyond).start()
        for k in range(PLANE):
            block(ACROSS, k, across).start()
        for k in range(PLANE):
            fill_relay(1, k)
            relayed(RELAY_OUT, k, 1, out_plane).start()
        for k in range(1, PLANE):
            fill_relay(0, k)
            relayed(RELAY_OWN, k, 0, plane).start()
        fill_relay(0, 0)
        own_relay.start()
        own_relay.wait()
        for k in range(PLANE):
            block(BEYOND, k, beyond).wait_send()
            block(OUT, k, out_plane).wait_send()
            relayed(RELAY_OUT, k, 1, out_plane).wait_send()
            block(ACROSS, k, across).wait()
            block(INWARD, k, plane).wait_recv()
        for k in range(1, PLANE):
            relayed(RELAY_OWN, k, 0, plane).wait()

    own.wait()
    for k in range(1, PLANE):
        block(OWN, k, plane).wait()


def tell_kernel(asked_ref, told_ref, send, recv):
    me, plane, spot = here()
    count = told_ref.shape[0]
    store, head = me // 2, me % 2
    barrier = pltpu.get_barrier_semaphore()

    def greet(k, carry):
        pl.semaphore_signal(
            barrier,
            inc=1,
            device_id={"store": (store + k) % count},
            device_id_type=pl.DeviceIdType.MESH,
        )
        return carry

    lax.fori_loop(1, count, greet, 0)
    told_ref[store] = asked_ref[...]
    pl.semaphore_wait(barrier, count - 1)

    def table(k):
        peer = (store + k) % count * 2 + head
        return remote(asked_ref, told_ref.at[store], send.at[k], recv.at[k], peer)

    for k in range(1, count):
        table(k).start()
    for k in range(1, count):
        table(k).wait()


def tell(asked, store_count):
    table = jnp.pad(asked, ((0, 0), (0, 128 - asked.shape[1])))
    told = pl.pallas_call(
        tell_kernel,
        out_shape=jax.ShapeDtypeStruct((store_count,) + table.shape, jnp.int32),
        in_specs=[pl.BlockSpec(memory_space=pltpu.VMEM)],
        out_specs=pl.BlockSpec(memory_space=pltpu.VMEM),
        scratch_shapes=[pltpu.SemaphoreType.DMA((store_count,))] * 2,
        compiler_params=pltpu.CompilerParams(collective_id=3, has_side_effects=True),
    )(table)
    return told[:, :, : asked.shape[1]]


def exchange(wanted_all, passage_kv):
    any_space = pl.BlockSpec(memory_space=pl.ANY)
    me, plane, spot = here()
    origin = jnp.where(plane == 2, 0, 3) * PLANE + spot
    for_origin = lax.dynamic_index_in_dim(wanted_all, origin, 1, keepdims=False)
    cap = for_origin.shape[1]
    by_plane = for_origin.reshape(4, 2, cap)
    out_plane = jnp.where(plane == 1, 0, 3)
    lists = jnp.concatenate(
        [
            lax.dynamic_index_in_dim(by_plane, plane, 0, keepdims=False),
            lax.dynamic_index_in_dim(by_plane, out_plane, 0, keepdims=False),
        ],
        axis=0,
    )
    lists = jnp.concatenate([wanted_all[:, me], lists], axis=0)
    lists = jnp.repeat(lists, 2, axis=0).reshape(-1)
    blocks = (4 * PLANE, cap, 2, PLEN, passage_kv.shape[3] // 2)
    return pl.pallas_call(
        exchange_kernel,
        out_shape=jax.ShapeDtypeStruct(blocks, jnp.bfloat16),
        in_specs=[pl.BlockSpec(memory_space=pltpu.SMEM), any_space],
        out_specs=any_space,
        scratch_shapes=[
            pltpu.VMEM(passage_kv.shape, jnp.bfloat16),
            pltpu.VMEM(blocks, jnp.bfloat16),
            pltpu.VMEM(passage_kv.shape, jnp.bfloat16),
            pltpu.VMEM((2, PLANE) + blocks[1:], jnp.bfloat16),
            pltpu.SemaphoreType.DMA((7 * PLANE + 1,)),
            pltpu.SemaphoreType.DMA((7 * PLANE + 1,)),
            pltpu.SemaphoreType.DMA((3,)),
        ],
        compiler_params=pltpu.CompilerParams(
            collective_id=1, has_side_effects=True, vmem_limit_bytes=VMEM_LIMIT
        ),
    )(lists, passage_kv)


def local(queries, own_keys, own_values, passage_kv, passage_rows, retrieval, offsets):
    stored_count = passage_kv.shape[0]
    store_count = lax.axis_size("store")
    head_count = lax.axis_size("head")
    peer_count = store_count * head_count
    requests = queries.shape[0]
    pick_ids = retrieval.reshape(-1)
    pick_count = pick_ids.shape[0]
    cap_dev = 3 * pick_count // (2 * peer_count)
    store_rows = passage_rows[pick_ids]
    owner_dev = store_rows // stored_count
    local_row = store_rows % stored_count
    slot_index = owner_dev * cap_dev + ranks_within(owner_dev)
    asked = request_table(slot_index, local_row, peer_count * cap_dev).reshape(peer_count, cap_dev)
    relays = store_count == 8 and head_count == 2 and 2 * cap_dev >= stored_count
    if relays:
        wanted_all = tell(asked, store_count)
    else:
        wanted = lax.all_to_all(asked, ("store", "head"), split_axis=0, concat_axis=0, tiled=True)
        outgoing = pack(wanted, passage_kv, store_count, head_count, cap_dev, CHUNKS)

    turn_by = jnp.arange(pick_count, dtype=jnp.int32) % NPASS * PLEN - offsets[pick_ids]
    half_dim = HEAD_DIM // 2
    inverse_freq = rope_theta ** (-(jnp.arange(half_dim, dtype=jnp.float32) * 2.0) / HEAD_DIM)
    angles = turn_by.astype(jnp.float32)[:, None] * inverse_freq[None, :]
    cosine, sine = jnp.cos(angles), jnp.sin(angles)
    cosine = jnp.concatenate([cosine, cosine], axis=1).reshape(requests, NPASS, HEAD_DIM)
    sine = jnp.concatenate([-sine, sine], axis=1).reshape(requests, NPASS, HEAD_DIM)

    result = None
    for chunk in range(CHUNKS):
        if relays:
            incoming = exchange(wanted_all, passage_kv)
        else:
            incoming = lax.all_to_all(
                outgoing[chunk], ("store", "head"), split_axis=0, concat_axis=0, tiled=True
            )
        fetched = incoming.reshape((peer_count * cap_dev,) + incoming.shape[2:])
        result = attend(
            chunk, CHUNKS, slot_index, queries, own_keys, own_values, cosine, sine, fetched, result
        )
    return result


def solution(mesh):
    in_specs = (
        P(("parts", "store"), None, "head"),
        P(("parts", "store"), None, "head"),
        P(("parts", "store"), None, "head"),
        P(("parts", "store", "head"), None, None, None),
        P("parts"),
        P(("parts", "store"), None),
        P("parts"),
    )
    out_specs = P(("parts", "store"), None, "head")
    return jax.shard_map(local, mesh=mesh, in_specs=in_specs, out_specs=out_specs, check_vma=False)
```
